768 devices in a mesh: dp: 96 (over x, z, core), owner: 8 (over y).
Axes of the slice: x: 4, y: 8, z: 12, core: 2. Of those that a mesh axis runs over, the one named last changes fastest.
Arguments:
- grad_parts: bfloat16 [96, 192, 256, 256], P('dp', None, 'owner'), may hold values from -3 to 3
- stats_in: float32 [96, 16, 256, 256], P('dp', 'owner'), may hold values from -16 to 8192, as said below
- assignment: int32 [96, 4, 1], P('dp'), may hold values from 0 to 7; in each aligned block of 4 rows (0 to 3, 4 to 7, ..., all dimensions but the last counted through in order) at most 2 rows name the same one
Outputs:
- update: bfloat16 [192, 256, 256], P('dp', 'owner')
- stats_out: float32 [96, 16, 256, 256], P('dp', 'owner')
The draws below stay inside these ranges and needn't reach their ends.
Inputs may be any that keep to these rules, and one draw needn't show every extreme that they name: `assignment`: in each dp index's 4 tasks no owner index is named more than 2 times. Every 256 x 256 matrix of stats_in is symmetric positive definite.
All inputs are finite; a program needn't handle non-finite values.
Results may differ from the reference program's by a relative error of at most 0.0069.
Values may be sent and summed in bfloat16 or wider, within the bound.
A program may use at most 32 MiB of HBM per device.

```python
import math
import jax
import jax.numpy as jnp
import numpy as np
from jax import lax

BS = 256
BLK_ROW = 2
CAP = 2
NEWTON = 2
TASKS = 4
NBLK = 192
N_DP = 96
N_OWNER = 8


def draw_grad_parts(key, part):
    key = jax.random.fold_in(key, 11)
    key_rows, key_cols, key_vals = jax.random.split(key, 3)
    row_scale = jnp.exp(jax.random.uniform(key_rows, (NBLK, BS, 1), jnp.float32, 0.0, math.log(10.0)))
    row_trend = jnp.exp(math.log(3.0) * (jnp.arange(BS, dtype=jnp.float32) / BS - 1.0))[None, :, None]
    col_scale = jnp.exp(jax.random.uniform(key_cols, (NBLK, 1, BS), jnp.float32, -0.5 * math.log(10.0), 0.5 * math.log(10.0)))
    scales = row_scale * row_trend * col_scale * (0.2 / math.sqrt(N_DP))
    values = jax.random.truncated_normal(key_vals, -4.0, 4.0, (N_DP, NBLK, BS, BS), jnp.float32)
    return jnp.clip(values * scales[None], -3.0, 3.0).astype(jnp.bfloat16)


def draw_stats_in(key, part):
    key = jax.random.fold_in(key, 23)
    key_off, key_diag, key_factor = jax.random.split(key, 3)
    full_shape = (N_DP, CAP * N_OWNER, BS, BS)
    uniform_part = jax.random.uniform(key_off, full_shape, jnp.float32, -1.0, 1.0)
    off_diag = 0.5 * (uniform_part + jnp.swapaxes(uniform_part, 2, 3))
    unit_diag = jnp.eye(BS, dtype=jnp.float32)
    diag_values = BS * (1.0 + jax.random.uniform(key_diag, full_shape[:3], jnp.float32, 0.0, 1.0))
    row_factor = jnp.exp(jax.random.uniform(key_factor, full_shape[:3], jnp.float32, 0.0, 0.5 * math.log(10.0)))
    matrix = off_diag * (1.0 - unit_diag) + unit_diag * diag_values[..., None]
    return matrix * row_factor[..., :, None] * row_factor[..., None, :]


def deal_out(rng, own, number, rows, amount, top, reach, lean):
    ranking = jax.random.permutation(rng, amount)
    heavy_load, usual = portions_of(amount, rows * top, reach, lean, True), portions_of(amount, rows * top, reach, lean, False)
    places = jnp.arange(amount)

    def named(lengths, turn):
        used = int((lengths > 0).sum())
        fixed = max(1, used // 4)
        moved = fixed + (places - fixed + turn * (used - fixed)) % max(1, amount - fixed)
        return jnp.zeros((amount,), jnp.int32).at[ranking[jnp.where(places < fixed, places, moved)]].set(jnp.asarray(lengths, jnp.int32))

    lengths = jnp.where(number % 4 == 0, named(heavy_load, number // 4), named(usual, number - number // 4 - 1))
    mixed = jax.random.permutation(jax.random.fold_in(own, 3), amount)
    giver, receiver = mixed[0:amount // 2 * 2:2], mixed[1:amount // 2 * 2:2]
    slack = jnp.minimum(lengths[giver] - 1, reach - lengths[receiver]) // 2
    slack = jnp.where((giver == ranking[0]) | (receiver == ranking[0]) | (lengths[receiver] == 0), 0, jnp.maximum(slack, 0))
    moved = jax.random.randint(jax.random.fold_in(own, 4), (amount // 2,), 0, 1 << 20) % (slack + 1)
    lengths = lengths.at[giver].add(-moved).at[receiver].add(moved)
    members = jnp.searchsorted(jnp.cumsum(lengths), jnp.arange(rows * top), side="right").astype(jnp.int32)
    listing = members.reshape(top, rows).T
    listing = listing[jax.random.permutation(jax.random.fold_in(own, 1), rows)]
    turn = jax.random.randint(jax.random.fold_in(own, 2), (rows, 1), 0, top)
    return jnp.take_along_axis(listing, (jnp.arange(top)[None, :] + turn) % top, axis=1)


def portions_of(number_of, total, bound, skew, full):
    weights = [(1 << 20) // math.isqrt(rank ** skew) + 1 for rank in range(1, number_of + 1)]
    largest = bound if full else min(bound, max(-(-total // number_of), total * weights[0] // sum(weights)))
    least = 1 if total - largest >= number_of - 1 else 0
    holding, rest = [largest] + [least] * (number_of - 1), total - largest - least * (number_of - 1)
    while rest > 0:
        candidates = [i for i in range(1, number_of) if holding[i] < largest] or [i for i in range(1, number_of) if holding[i] < bound]
        pool, remaining = sum([weights[i] for i in candidates]), rest
        for i in candidates:
            addition = min(bound - holding[i], max(1, remaining * weights[i] // pool), rest)
            holding[i] = holding[i] + addition
            rest = rest - addition
    return np.array(holding)


def setup_inputs(seed: int = 0) -> dict:
    seeds = jax.random.split(jax.random.key(seed), 4)
    grad_parts = draw_grad_parts(jax.random.fold_in(seeds[3], 71), 0)
    stats_in = draw_stats_in(jax.random.fold_in(seeds[3], 71), 0)
    assignment_keys = jax.random.split(jax.random.fold_in(seeds[2], 1), N_DP * TASKS // TASKS)
    assignment_turns = jax.random.permutation(jax.random.fold_in(seeds[2], 3), N_DP * TASKS // TASKS)
    assignment = jax.vmap(lambda own, number: deal_out(jax.random.fold_in(seeds[2], 2), own, number, TASKS, N_OWNER, 1, CAP, 2))(assignment_keys, assignment_turns).reshape((N_DP, TASKS, 1))
    return {"grad_parts": grad_parts, "stats_in": stats_in, "assignment": assignment}


DECAY_RATE = 0.95
NORM_EPSILON = 1e-06

def matmul_high(left_side, right_side):
    return jnp.matmul(left_side, right_side, precision=lax.Precision.HIGHEST)

def slot_table(owner_list):
    positions = jnp.arange(owner_list.shape[0], dtype=jnp.int32)
    same_owner = owner_list[:, None] == owner_list[None, :]
    earlier = positions[None, :] < positions[:, None]
    slot_rank = lax.optimization_barrier(jnp.sum(jnp.logical_and(same_owner, earlier).astype(jnp.int32), axis=1))
    return owner_list * CAP + slot_rank

def inverse_root(stats_all):
    identity = jnp.eye(stats_all.shape[-1], dtype=jnp.float32)
    norm_value = jnp.sqrt(lax.optimization_barrier(jnp.sum(stats_all * stats_all, axis=(1, 2), keepdims=True)) + NORM_EPSILON)
    matrix = stats_all / norm_value
    current = jnp.broadcast_to(identity, matrix.shape)
    for iteration in range(NEWTON):
        factor = (5.0 * identity - matrix) * 0.25
        current = matmul_high(current, factor)
        square = matmul_high(factor, factor)
        matrix = matmul_high(matmul_high(square, square), matrix)
    return current.astype(jnp.bfloat16)

def row_work(inputs):
    blocks, stats_row, row_assign = inputs
    owner_list = row_assign[:, 0].astype(jnp.int32)
    slots = slot_table(owner_list)
    task_ids = jnp.arange(TASKS, dtype=jnp.int32)
    selected = blocks[task_ids // 2]
    oriented = jnp.where((task_ids % 2)[:, None, None] == 1, jnp.swapaxes(selected, 1, 2), selected)
    oriented_wide = oriented.astype(jnp.float32)
    gram_matrix = jnp.einsum('tik,tjk->tij', oriented_wide, oriented_wide)
    task_stats = DECAY_RATE * stats_row[slots] + gram_matrix
    stats_new = jnp.zeros((CAP * N_OWNER, BS, BS), jnp.float32).at[slots].set(task_stats)
    roots = inverse_root(task_stats)
    left_roots = roots[0::2].astype(jnp.float32)
    right_roots = roots[1::2].astype(jnp.float32)
    blocks_wide = blocks.astype(jnp.float32)
    half_product = jnp.einsum('jik,jkl->jil', left_roots, blocks_wide).astype(jnp.bfloat16)
    preconditioned = jnp.einsum('jik,jkl->jil', half_product.astype(jnp.float32), right_roots)
    grad_squares = lax.optimization_barrier(jnp.sum(blocks_wide * blocks_wide, axis=(1, 2)))
    pre_squares = lax.optimization_barrier(jnp.sum(preconditioned * preconditioned, axis=(1, 2)))
    graft_scale = jnp.sqrt(grad_squares + NORM_EPSILON) / jnp.sqrt(pre_squares + NORM_EPSILON)
    update = (preconditioned * graft_scale[:, None, None]).astype(jnp.bfloat16)
    return (update, stats_new)

def reference(grad_parts, stats_in, assignment):

    def accumulate(running, replica):
        return (running + replica.astype(jnp.float32), None)
    summed, unused = lax.scan(accumulate, jnp.zeros(grad_parts.shape[1:], jnp.float32), grad_parts)
    gradient = summed.astype(jnp.bfloat16)
    row_blocks = gradient.reshape(N_DP, BLK_ROW, BS, BS)
    updates, stats_out = lax.map(row_work, (row_blocks, stats_in, assignment))
    return (updates.reshape(NBLK, BS, BS), stats_out)
```

```python
import functools

import jax
import jax.numpy as jnp
from jax import lax
from jax.experimental import pallas as pl
from jax.experimental.pallas import tpu as pltpu
from jax.sharding import PartitionSpec as P

NX, NZ, NC, NY = 4, 12, 2, 8
BLOCKS = 2
TASKS = 4
CAP = 2
BS = 256
ROWS = BS // NY
HALF = ROWS // 2
FAR = 5
DECAY_RATE = 0.95
NORM_EPSILON = 1e-06
MESH = pl.DeviceIdType.MESH
F32 = jnp.float32
BF16 = jnp.bfloat16

Z_ORDER = [(6 + (1 - 2 * (q % 2)) * ((q + 1) // 2)) % NZ for q in range(NZ)]

CORE = 0
X_OPP = CORE + NX * BLOCKS
X_A = X_OPP + 2 * BLOCKS
X_BF = X_A + 2 * BLOCKS
X_BN = X_BF + 2 * BLOCKS
Z_FAR = X_BN + 2 * BLOCKS
Z_NEAR = Z_FAR + 6 * BLOCKS
Y_SLOT = Z_NEAR + 6 * BLOCKS
Y_TASK = Y_SLOT + NY
Y_GRAD = Y_TASK + NY
N_SEMS = Y_GRAD + NY * BLOCKS
L_OWN = 0
L_STATS = L_OWN + NX * BLOCKS
L_OUT = L_STATS + 1
N_LOCAL = L_OUT + 2


def dot(left, right, dims=((1,), (0,))):
    return lax.dot_general(left, right, (dims, ((), ())), preferred_element_type=F32)


def inverse_root(stats):
    scale = 0.25 * lax.rsqrt(jnp.sum(stats * stats) + NORM_EPSILON)
    quarter = stats * scale
    quarter16 = quarter.astype(BF16)
    excess = dot(quarter16, quarter16) - 2.5 * quarter
    excess16 = excess.astype(BF16)
    fourth = (3.125 * excess + dot(excess16, excess16)).astype(BF16)
    carried = 2.44140625 * quarter + dot(fourth, quarter16)
    rows = lax.broadcasted_iota(jnp.int32, (BS, BS), 0)
    columns = lax.broadcasted_iota(jnp.int32, (BS, BS), 1)
    diagonal = jnp.where(rows == columns, F32(1.5625), F32(0.0))
    root = diagonal - 1.25 * (quarter + carried) + dot(quarter16, carried.astype(BF16))
    return root.astype(BF16)


def kernel(parts, stats_in, assign, update, stats_out,
           own, other, chip, rx_opp, rx_a, rx_b, tx_b, xs, xs_own, rz6, rz54, tx_z, rz_near,
           grad, slots_in, slots16, slot_rows, task_stats, gram, new_stats, pre_ref, upd_rows,
           send_sems, recv_sems, local_sems):
    dp = lax.axis_index("dp")
    y = lax.axis_index("owner")
    x, z, core = dp // (NZ * NC), (dp // NC) % NZ, dp % NC

    def device(dx=0, dz=0, dc=0, dy=0):
        return (
            (((x + dx + NX) % NX) * NZ + (z + dz + NZ) % NZ) * NC + (core + dc) % NC,
            (y + dy + NY) % NY,
        )

    sent = []

    def send(src, dst, number, target):
        copy = pltpu.make_async_remote_copy(
            src_ref=src, dst_ref=dst, send_sem=send_sems.at[number], recv_sem=recv_sems.at[number],
            device_id=target, device_id_type=MESH,
        )
        copy.start()
        sent.append(copy)
        return copy

    own_loads = {}
    for j in range(BLOCKS):
        for k in (2, 1, 3, 0):
            copy = pltpu.make_async_copy(
                parts.at[(x + k) % NX, :, core, j], own.at[k, j], local_sems.at[L_OWN + k * BLOCKS + j]
            )
            own_loads[k, j] = copy
    stats_load = pltpu.make_async_copy(stats_in, slots_in, local_sems.at[L_STATS])

    partners = [device(dc=1), device(dx=1), device(dx=-1)]
    partners += [device(dz=d) for d in (1, 2, 3, -1, -2, -3)]
    partners += [device(dy=d) for d in range(1, NY)]
    barrier = pltpu.get_barrier_semaphore()
    for partner in partners:
        pl.semaphore_signal(barrier, inc=1, device_id=partner, device_id_type=MESH)
    stats_load.start()
    for copy in own_loads.values():
        copy.start()
    stats_load.wait()
    slots16[...] = slots_in[...].astype(BF16)
    pl.semaphore_wait(barrier, len(partners))

    core_copies = {}
    for j in range(BLOCKS):
        for k in (2, 1, 3, 0):
            core_copies[k, j] = send(
                parts.at[(x + k) % NX, :, 1 - core, j], other.at[k, j], CORE + k * BLOCKS + j, device(dc=1)
            )

    my_rows = pl.ds(pl.multiple_of(y * ROWS, ROWS), ROWS)
    slot_copies = []
    for d in (4, 3, 5, 2, 6, 1, 7):
        target_rows = pl.ds(pl.multiple_of(((y + d) % NY) * ROWS, ROWS), ROWS)
        slot_copies.append(
            send(slots16.at[:, target_rows], slot_rows.at[y], Y_SLOT + d, device(dy=d))
        )
    slot_rows[y] = slots16[:, my_rows]

    def chip_sum(k, j):
        own_loads[k, j].wait()
        core_copies[k, j].wait_recv()

        def step(q, carry):
            place = (z + 6 + (1 - 2 * (q % 2)) * ((q + 1) // 2)) % NZ
            total = own[k, j, place].astype(F32) + other[k, j, place].astype(F32)
            chip[k, j, q] = total.astype(BF16)
            return carry

        lax.fori_loop(0, NZ, step, 0)

    low, high = pl.ds(0, HALF), pl.ds(HALF, HALF)
    far, near = pl.ds(0, FAR), pl.ds(FAR, NZ - FAR)
    x_opp, x_a, x_bf, x_bn = {}, {}, {}, {}

    def send_opposite(j):
        x_opp[0, j] = send(chip.at[2, j, :, low], rx_opp.at[0, j], X_OPP + j, device(dx=1))
        x_opp[1, j] = send(chip.at[2, j, :, high], rx_opp.at[1, j], X_OPP + BLOCKS + j, device(dx=-1))

    def send_a(j):
        x_a[0, j] = send(chip.at[1, j, :, high], rx_a.at[0, j], X_A + j, device(dx=1))
        x_a[1, j] = send(chip.at[3, j, :, low], rx_a.at[1, j], X_A + BLOCKS + j, device(dx=-1))

    def send_b(j):
        for side, (k, part, step) in enumerate(((1, low, 1), (3, high, -1))):
            x_opp[side, j].wait_recv()
            for places, copies, base in ((far, x_bf, X_BF), (near, x_bn, X_BN)):
                total = chip[k, j, places, part].astype(F32) + rx_opp[side, j, places].astype(F32)
                tx_b[side, j, places] = total.astype(BF16)
                copies[side, j] = send(
                    tx_b.at[side, j, places], rx_b.at[side, j, places], base + side * BLOCKS + j, device(dx=step)
                )

    chip_sum(2, 0)
    send_opposite(0)
    chip_sum(1, 0)
    chip_sum(3, 0)
    send_a(0)
    chip_sum(2, 1)
    send_opposite(1)
    send_b(0)
    chip_sum(0, 0)
    chip_sum(1, 1)
    chip_sum(3, 1)
    send_a(1)
    send_b(1)
    chip_sum(0, 1)

    owners = [assign[t] for t in range(TASKS)]
    ranks = [
        sum(((owners[s] == owners[t]).astype(jnp.int32) for s in range(t)), jnp.int32(0)) for t in range(TASKS)
    ]
    for copy in slot_copies:
        copy.wait_recv()
    for t in range(TASKS):
        task_stats[t, my_rows] = slot_rows[owners[t], jnp.minimum(ranks[t], CAP - 1)]
    task_copies = [
        send(task_stats.at[:, my_rows], task_stats.at[:, my_rows], Y_TASK + d, device(dy=d))
        for d in (4, 3, 5, 2, 6, 1, 7)
    ]

    def x_total(j, places):
        bottom = chip[0, j, places, low].astype(F32) + rx_b[0, j, places].astype(F32) + rx_a[1, j, places].astype(F32)
        top = chip[0, j, places, high].astype(F32) + rx_a[0, j, places].astype(F32) + rx_b[1, j, places].astype(F32)
        return bottom, top

    z_far, z_near = {}, {}

    def far_stage(j):
        for side in range(2):
            x_a[side, j].wait_recv()
            x_bf[side, j].wait_recv()
        bottom, top = x_total(j, far)
        xs[j, far, low] = bottom.astype(BF16)
        xs[j, far, high] = top.astype(BF16)
        base = Z_FAR + 6 * j
        z_far[j] = [
            send(xs.at[j, 0, low], rz6.at[0, j], base, device(dz=3)),
            send(xs.at[j, 0, high], rz6.at[1, j], base + 1, device(dz=-3)),
            send(xs.at[j, 1], rz54.at[0, j, 0], base + 2, device(dz=2)),
            send(xs.at[j, 2], rz54.at[1, j, 0], base + 3, device(dz=-2)),
            send(xs.at[j, 3], rz54.at[0, j, 1], base + 4, device(dz=1)),
            send(xs.at[j, 4], rz54.at[1, j, 1], base + 5, device(dz=-1)),
        ]

    def near_stage(j):
        for side in range(2):
            x_bn[side, j].wait_recv()
        bottom, top = x_total(j, near)
        xs[j, near, low] = bottom.astype(BF16)
        xs[j, near, high] = top.astype(BF16)
        xs_own[j, low] = bottom[NZ - FAR - 1]
        xs_own[j, high] = top[NZ - FAR - 1]
        base = Z_NEAR + 6 * j
        z_near[j] = [
            send(xs.at[j, 7], rz_near.at[j, 2], base + 2, device(dz=2)),
            send(xs.at[j, 8], rz_near.at[j, 3], base + 3, device(dz=-2)),
            send(xs.at[j, 9], rz_near.at[j, 4], base + 4, device(dz=1)),
            send(xs.at[j, 10], rz_near.at[j, 5], base + 5, device(dz=-1)),
        ]

    def relay_stage(j):
        for copy in z_far[j]:
            copy.wait_recv()
        base = Z_NEAR + 6 * j
        for side, (part, rest, step) in enumerate(((low, high, 3), (high, low, -3))):
            total = (
                xs[j, 5 + side].astype(F32) + rz54[side, j, 0].astype(F32) + rz54[side, j, 1].astype(F32)
            )
            split = total[:HALF] if side == 0 else total[HALF:]
            plain = total[HALF:] if side == 0 else total[:HALF]
            tx_z[side, j, part] = (split + rz6[side, j].astype(F32)).astype(BF16)
            tx_z[side, j, rest] = plain.astype(BF16)
            z_near[j].append(send(tx_z.at[side, j], rz_near.at[j, side], base + side, device(dz=step)))

    grad_copies = {}

    def grad_stage(j):
        for copy in z_near[j]:
            copy.wait_recv()
        total = xs_own[j]
        for n in range(6):
            total = total + rz_near[j, n].astype(F32)
        grad[j, my_rows] = total.astype(BF16)
        grad_copies[j] = [
            send(grad.at[j, my_rows], grad.at[j, my_rows], Y_GRAD + NY * j + d, device(dy=d))
            for d in (4, 3, 5, 2, 6, 1, 7)
        ]

    far_stage(0)
    near_stage(0)
    far_stage(1)
    relay_stage(0)
    near_stage(1)
    relay_stage(1)
    grad_stage(0)
    grad_stage(1)

    for copy in task_copies:
        copy.wait_recv()
    for j in range(BLOCKS):
        for copy in grad_copies[j]:
            copy.wait_recv()
        block = grad[j]
        gram[2 * j] = dot(block, block, ((1,), (1,)))
        gram[2 * j + 1] = dot(block, block, ((0,), (0,)))
        left = inverse_root(DECAY_RATE * task_stats[2 * j].astype(F32) + gram[2 * j])
        right = inverse_root(DECAY_RATE * task_stats[2 * j + 1].astype(F32) + gram[2 * j + 1])
        half = dot(left, block).astype(BF16)
        pre = dot(half, right)
        pre_ref[...] = pre
        wide = block.astype(F32)
        scale = jnp.sqrt(jnp.sum(wide * wide) + NORM_EPSILON) / jnp.sqrt(jnp.sum(pre * pre) + NORM_EPSILON)
        upd_rows[j] = (pre_ref[my_rows] * scale).astype(BF16)

    for c in range(CAP):
        matches = [
            jnp.logical_and(owners[t] == y, ranks[t] == c).astype(jnp.int32) for t in range(TASKS)
        ]
        used = sum(matches, jnp.int32(0))
        task = sum((t * matches[t] for t in range(TASKS)), jnp.int32(0))
        fresh = DECAY_RATE * slots_in[c] + gram[jnp.minimum(task, TASKS - 1)]
        new_stats[c] = jnp.where(used > 0, fresh, jnp.zeros_like(fresh))
    out_copies = [
        pltpu.make_async_copy(new_stats, stats_out, local_sems.at[L_OUT]),
        pltpu.make_async_copy(upd_rows, update, local_sems.at[L_OUT + 1]),
    ]
    for copy in out_copies:
        copy.start()
    for copy in sent:
        copy.wait_send()
    for copy in out_copies:
        copy.wait()


def per_device(grad_parts, stats_in, assignment):
    parts = grad_parts.reshape(NX, NZ, NC, BLOCKS, ROWS, BS)
    slots = stats_in[0]
    assign = assignment.reshape(TASKS)
    any_space = pl.BlockSpec(memory_space=pl.ANY)
    update, stats_out = pl.pallas_call(
        kernel,
        out_shape=(
            jax.ShapeDtypeStruct((BLOCKS, ROWS, BS), BF16),
            jax.ShapeDtypeStruct((CAP, BS, BS), F32),
        ),
        in_specs=[any_space, any_space, pl.BlockSpec(memory_space=pltpu.SMEM)],
        out_specs=(any_space, any_space),
        scratch_shapes=[
            pltpu.VMEM((NX, BLOCKS, NZ, ROWS, BS), BF16),
            pltpu.VMEM((NX, BLOCKS, NZ, ROWS, BS), BF16),
            pltpu.VMEM((NX, BLOCKS, NZ, ROWS, BS), BF16),
            pltpu.VMEM((2, BLOCKS, NZ, HALF, BS), BF16),
            pltpu.VMEM((2, BLOCKS, NZ, HALF, BS), BF16),
            pltpu.VMEM((2, BLOCKS, NZ, HALF, BS), BF16),
            pltpu.VMEM((2, BLOCKS, NZ, HALF, BS), BF16),
            pltpu.VMEM((BLOCKS, NZ, ROWS, BS), BF16),
            pltpu.VMEM((BLOCKS, ROWS, BS), F32),
            pltpu.VMEM((2, BLOCKS, HALF, BS), BF16),
            pltpu.VMEM((2, BLOCKS, 2, ROWS, BS), BF16),
            pltpu.VMEM((2, BLOCKS, ROWS, BS), BF16),
            pltpu.VMEM((BLOCKS, 6, ROWS, BS), BF16),
            pltpu.VMEM((BLOCKS, BS, BS), BF16),
            pltpu.VMEM((CAP, BS, BS), F32),
            pltpu.VMEM((CAP, BS, BS), BF16),
            pltpu.VMEM((NY, CAP, ROWS, BS), BF16),
            pltpu.VMEM((TASKS, BS, BS), BF16),
            pltpu.VMEM((TASKS, BS, BS), F32),
            pltpu.VMEM((CAP, BS, BS), F32),
            pltpu.VMEM((BS, BS), F32),
            pltpu.VMEM((BLOCKS, ROWS, BS), BF16),
            pltpu.SemaphoreType.DMA((N_SEMS,)),
            pltpu.SemaphoreType.DMA((N_SEMS,)),
            pltpu.SemaphoreType.DMA((N_LOCAL,)),
        ],
        compiler_params=pltpu.CompilerParams(
            collective_id=0, has_side_effects=True, vmem_limit_bytes=60 * 1024 * 1024
        ),
        name="shampoo_step",
    )(parts, slots, assign)
    return update, stats_out[None]


def solution(mesh):
    in_specs = (P("dp", None, "owner", None), P("dp", "owner", None, None), P("dp", None, None))
    out_specs = (P("dp", "owner", None), P("dp", "owner", None, None))
    return jax.shard_map(
        per_device, mesh=mesh, in_specs=in_specs, out_specs=out_specs, check_vma=False
    )
```

```python
import jax
import jax.numpy as jnp
from jax import lax
from jax.experimental import pallas as pl
from jax.experimental.pallas import tpu as pltpu
from jax.sharding import PartitionSpec as P

NX, NZ, NC, NY = 4, 12, 2, 8
BLOCKS = 2
TASKS = 4
CAP = 2
BS = 256
MID = BS // 2
ROWS = BS // NY
HALF = ROWS // 2
FAR = 5
DECAY_RATE = 0.95
NORM_EPSILON = 1e-06
MESH = pl.DeviceIdType.MESH
F32 = jnp.float32
BF16 = jnp.bfloat16

Z_ORDER = (6, 5, -5, 4, -4, 3, -3, 2, -2, 1, -1, 0)
Y_ORDER = (4, 3, 5, 2, 6, 1, 7)
UNITS = 4
X_UNITS = 3
LAST = UNITS - 1
GROUPS = (pl.ds(0, 2), pl.ds(2, 1))
CORE_ORDER = ((1, True), (3, True), (0, True), (1, False), (3, False), (0, False))

R_CORE_FAR, R_CORE_NEAR, R_X_FAR, R_X_NEAR, R_Z6, R_Z54, R_Z_NEAR, R_SLOT_TOP, R_SLOT_LOW = 0, 4, 8, 9, 11, 12, 13, 15, 16
R_TASK_TOP, R_TASK_LOW, R_GRAD, R_W6, R_W54, R_W_NEAR, R_W_X = 17, 18, 19, 21, 22, 23, 24
N_RECV = 25
S_CORE, S_X, S_Z6, S_Z54, S_SLOT_TOP, S_SLOT_LOW, S_TASK_TOP, S_TASK_LOW, S_GRAD, S_W6, S_W54, S_W_NEAR, S_W_X = range(13)
S_Z_NEAR = 13
N_SEND = 15
L_OWN_FAR, L_OWN_NEAR, L_STATS, L_STATS_OUT, L_UPDATE, L_ASSIGN = 0, 4, 8, 9, 10, 11
N_LOCAL = 12
IN_X, IN_Y, IN_Z = 0, 1, 4
N_IN = 6


def dot(left, right, dims=((1,), (0,))):
    return lax.dot_general(left, right, (dims, ((), ())), preferred_element_type=F32)


def inverse_root(stats):
    scale = 0.25 * lax.rsqrt(jnp.sum(stats * stats) + NORM_EPSILON)
    first = stats * scale
    first16 = first.astype(BF16)
    second = dot(first16, first16)
    second16 = second.astype(BF16)
    third = dot(first16, second16)
    third16 = third.astype(BF16)
    upper = dot((15.625 * first - 6.25 * second + third).astype(BF16), third16)
    rows = lax.broadcasted_iota(jnp.int32, (BS, BS), 0)
    columns = lax.broadcasted_iota(jnp.int32, (BS, BS), 1)
    diagonal = jnp.where(rows == columns, F32(1.5625), F32(0.0))
    root = diagonal - 4.3017578125 * first + 12.20703125 * second - 19.53125 * third + upper
    return root.astype(BF16)


def kernel(parts, stats_in, assign_in, update, stats_out,
           own, other, chip, rx_far, rx_near0, rx_near1,
           xs, xs_own, rz6, rz54, tx_z, rz_near0, rz_near1, rw6, rw54, tx_w, rw_near, ws, rw_x,
           grad, slots_in, slots16, slot_top, slot_low,
           task_top, task_low, task_stats, gram, new_stats, pre_ref, upd_rows,
           assign, send_sems, recv_sems, local_sems, in_sems):
    dp = lax.axis_index("dp")
    y = lax.axis_index("owner")
    x = dp // (NZ * NC)
    rest = dp - x * (NZ * NC)
    z = rest // NC
    core = rest - z * NC

    def around(position, step, size):
        moved = position + (step if step >= 0 else step + size)
        return moved - size * (moved >= size).astype(jnp.int32)

    x_at = [around(x, k, NX) for k in range(NX)]
    z_at = [around(z, step, NZ) for step in Z_ORDER]
    y_at = [around(y, d, NY) for d in range(NY)]

    def along_x(step):
        return (x_at[step % NX] * (NZ * NC) + rest, y)

    def along_z(step):
        return ((x * NZ + z_at[Z_ORDER.index(step)]) * NC + core, y)

    def along_y(d):
        return (dp, y_at[d])

    sibling = (dp + 1 - 2 * core, y)

    partners = [sibling, along_x(1), along_x(-1), along_z(1), along_z(-1), along_y(1), along_y(NY - 1)]
    barrier = pltpu.get_barrier_semaphore()
    for partner in partners:
        pl.semaphore_signal(barrier, inc=1, device_id=partner, device_id_type=MESH)

    def send(src, dst, send_number, recv_number, target):
        pltpu.make_async_remote_copy(
            src_ref=src, dst_ref=dst, send_sem=send_sems.at[send_number], recv_sem=recv_sems.at[recv_number],
            device_id=target, device_id_type=MESH,
        ).start()

    def wait(ref, sem):
        pltpu.make_async_copy(ref, ref, sem).wait()

    far, near = pl.ds(0, FAR), pl.ds(FAR, NZ - FAR)

    def load_own(k, is_far):
        base = L_OWN_FAR if is_far else L_OWN_NEAR
        for q in range(FAR) if is_far else range(FAR, NZ):
            pltpu.make_async_copy(
                parts.at[x_at[k], z_at[q], core], own.at[k, q], local_sems.at[base + k]
            ).start()

    def send_other(k, is_far):
        base = R_CORE_FAR if is_far else R_CORE_NEAR
        for q in range(FAR) if is_far else range(FAR, NZ):
            send(parts.at[x_at[k], z_at[q], 1 - core], other.at[k, q], S_CORE, base + k, sibling)

    def chip_sum(k, is_far):
        places = far if is_far else near
        wait(own.at[k, places], local_sems.at[(L_OWN_FAR if is_far else L_OWN_NEAR) + k])
        wait(other.at[k, places], recv_sems.at[(R_CORE_FAR if is_far else R_CORE_NEAR) + k])
        chip[k, places] = own[k, places] + other[k, places]

    load_own(2, True)
    stats_load = pltpu.make_async_copy(stats_in, slots_in, local_sems.at[L_STATS])
    stats_load.start()
    assign_load = pltpu.make_async_copy(assign_in, assign, local_sems.at[L_ASSIGN])
    assign_load.start()
    with jax.named_scope("barrier"):
        pl.semaphore_wait(barrier, len(partners))
    in_x = (along_x(1), along_x(-1))
    in_y = (along_y(1), along_y(NY - 1))
    in_z = (along_z(1), along_z(-1))

    def tell(number, neighbours):
        for neighbour in neighbours:
            pl.semaphore_signal(in_sems.at[number], inc=1, device_id=neighbour, device_id_type=MESH)

    def hear(number):
        pl.semaphore_wait(in_sems.at[number], 2)

    tell(IN_X, in_x)
    tell(IN_Y, in_y)
    tell(IN_Z, in_z)
    send_other(2, True)
    send_other(2, False)
    load_own(2, False)
    for k, is_far in CORE_ORDER:
        load_own(k, is_far)

    hear(IN_Y)
    tell(IN_Y + 1, in_y)
    hear(IN_Z)
    tell(IN_Z + 1, in_z)

    with jax.named_scope("chip_far"):
        chip_sum(2, True)
        for k, is_far in CORE_ORDER:
            send_other(k, is_far)
        hear(IN_X)
        send(chip.at[2, far, pl.ds(0, X_UNITS)], rx_far.at[0], S_X, R_X_FAR, along_x(2))
        chip_sum(1, True)
        send(chip.at[1, far, pl.ds(0, X_UNITS)], rx_far.at[1], S_X, R_X_FAR, along_x(1))
        chip_sum(3, True)
        send(chip.at[3, far, pl.ds(0, X_UNITS)], rx_far.at[2], S_X, R_X_FAR, along_x(-1))
        chip_sum(0, True)
    hear(IN_Y + 1)
    tell(IN_Y + 2, in_y)
    hear(IN_Z + 1)
    left, right = pl.ds(0, MID), pl.ds(MID, MID)
    with jax.named_scope("w_far"):
        for side, sign in enumerate((1, -1)):
            send(chip.at[:, 0, LAST, :, (left, right)[side]], rw6.at[side], S_W6, R_W6, along_z(3 * sign))
            send(chip.at[:, 1 + side, LAST], rw54.at[side, 0], S_W54, R_W54, along_z(2 * sign))
            send(chip.at[:, 3 + side, LAST], rw54.at[side, 1], S_W54, R_W54, along_z(sign))
    with jax.named_scope("chip_near"):
        chip_sum(2, False)
        chip_sum(1, False)
        chip_sum(3, False)
        for j, ref in enumerate((rx_near0, rx_near1)):
            for slot, k in enumerate((2, 1, 3)):
                send(chip.at[k, near, GROUPS[j]], ref.at[slot], S_X, R_X_NEAR + j, along_x(k if k < 3 else -1))
        chip_sum(0, False)
        for side, sign in enumerate((1, -1)):
            send(chip.at[:, 7 + side, LAST], rw_near.at[2 + side], S_W_NEAR, R_W_NEAR, along_z(2 * sign))
            send(chip.at[:, 9 + side, LAST], rw_near.at[4 + side], S_W_NEAR, R_W_NEAR, along_z(sign))
    hear(IN_Y + 2)

    my_eighth = pl.ds(pl.multiple_of(y * HALF, HALF), HALF)
    my_low = pl.ds(pl.multiple_of(MID + y * HALF, HALF), HALF)
    with jax.named_scope("slots"):
        stats_load.wait()
        slots16[...] = slots_in[...].astype(BF16)
        for d in Y_ORDER:
            top_rows = pl.ds(pl.multiple_of(y_at[d] * HALF, HALF), HALF)
            low_rows = pl.ds(pl.multiple_of(MID + y_at[d] * HALF, HALF), HALF)
            send(slots16.at[:, top_rows], slot_top.at[y], S_SLOT_TOP, R_SLOT_TOP, along_y(d))
            send(slots16.at[:, low_rows, right], slot_low.at[y], S_SLOT_LOW, R_SLOT_LOW, along_y(d))
        slot_top[y] = slots16[:, my_eighth]
        slot_low[y] = slots16[:, my_low, right]

    with jax.named_scope("z_far"):
        wait(rx_far, recv_sems.at[R_X_FAR])
        total = chip[0, far, pl.ds(0, X_UNITS)].astype(F32)
        for slot in range(3):
            total = total + rx_far[slot].astype(F32)
        xs[far] = total.astype(BF16)
        for side, sign in enumerate((1, -1)):
            send(xs.at[0, :, :, (left, right)[side]], rz6.at[side], S_Z6, R_Z6, along_z(3 * sign))
            send(xs.at[1 + side], rz54.at[side, 0], S_Z54, R_Z54, along_z(2 * sign))
            send(xs.at[3 + side], rz54.at[side, 1], S_Z54, R_Z54, along_z(sign))

    with jax.named_scope("w_relay"):
        wait(rw6, recv_sems.at[R_W6])
        wait(rw54, recv_sems.at[R_W54])
        for side, sign in enumerate((1, -1)):
            total = chip[:, 5 + side, LAST].astype(F32) + rw54[side, 0].astype(F32) + rw54[side, 1].astype(F32)
            part, other_part = (left, right) if side == 0 else (right, left)
            halves = (total[:, :, :MID], total[:, :, MID:])
            tx_w[side, :, :, part] = (halves[side] + rw6[side].astype(F32)).astype(BF16)
            tx_w[side, :, :, other_part] = halves[1 - side].astype(BF16)
            send(tx_w.at[side], rw_near.at[side], S_W_NEAR, R_W_NEAR, along_z(3 * sign))

    assign_load.wait()
    owners = [assign[t] for t in range(TASKS)]
    ranks = [
        sum(((owners[s] == owners[t]).astype(jnp.int32) for s in range(t)), jnp.int32(0)) for t in range(TASKS)
    ]
    with jax.named_scope("tasks"):
        wait(slot_top.at[pl.ds(0, NY - 1)], recv_sems.at[R_SLOT_TOP])
        wait(slot_low.at[pl.ds(0, NY - 1)], recv_sems.at[R_SLOT_LOW])
        for t in range(TASKS):
            rank = jnp.minimum(ranks[t], CAP - 1)
            task_top[t, my_eighth] = slot_top[owners[t], rank]
            task_low[t, my_eighth] = slot_low[owners[t], rank]
        for d in Y_ORDER:
            send(task_top.at[:, my_eighth], task_top.at[:, my_eighth], S_TASK_TOP, R_TASK_TOP, along_y(d))
            send(task_low.at[:, my_eighth], task_low.at[:, my_eighth], S_TASK_LOW, R_TASK_LOW, along_y(d))


    rz_near = (rz_near0, rz_near1)
    rx_near = (rx_near0, rx_near1)

    def z_near(j):
        wait(rx_near[j], recv_sems.at[R_X_NEAR + j])
        total = chip[0, near, GROUPS[j]].astype(F32)
        for slot in range(3):
            total = total + rx_near[j][slot].astype(F32)
        xs[near, GROUPS[j]] = total.astype(BF16)
        xs_own[GROUPS[j]] = total[NZ - FAR - 1]
        for side, sign in enumerate((1, -1)):
            send(xs.at[7 + side, GROUPS[j]], rz_near[j].at[2 + side], S_Z_NEAR + j, R_Z_NEAR + j, along_z(2 * sign))
            send(xs.at[9 + side, GROUPS[j]], rz_near[j].at[4 + side], S_Z_NEAR + j, R_Z_NEAR + j, along_z(sign))

    def z_relay():
        for side, sign in enumerate((1, -1)):
            total = xs[5 + side].astype(F32) + rz54[side, 0].astype(F32) + rz54[side, 1].astype(F32)
            part, other_part = (left, right) if side == 0 else (right, left)
            halves = (total[:, :, :MID], total[:, :, MID:])
            tx_z[side, :, :, part] = (halves[side] + rz6[side].astype(F32)).astype(BF16)
            tx_z[side, :, :, other_part] = halves[1 - side].astype(BF16)
        for j in range(BLOCKS):
            for side, sign in enumerate((1, -1)):
                send(tx_z.at[side, GROUPS[j]], rz_near[j].at[side], S_Z_NEAR + j, R_Z_NEAR + j, along_z(3 * sign))

    my_rows = pl.ds(pl.multiple_of(y * ROWS, ROWS), ROWS)
    my_last = pl.ds(pl.multiple_of(y * ROWS + HALF, HALF), HALF)

    def z_total(j):
        wait(rz_near[j], recv_sems.at[R_Z_NEAR + j])
        total = xs_own[GROUPS[j]]
        for n in range(6):
            total = total + rz_near[j][n].astype(F32)
        return total

    def gather(j):
        for d in Y_ORDER:
            send(grad.at[j, my_rows], grad.at[j, my_rows], S_GRAD, R_GRAD + j, along_y(d))

    with jax.named_scope("z_near0"):
        z_near(0)
    with jax.named_scope("z_near1"):
        z_near(1)
    with jax.named_scope("w_x"):
        wait(rw_near, recv_sems.at[R_W_NEAR])
        w_total = chip[:, NZ - 1, LAST].astype(F32)
        for n in range(6):
            w_total = w_total + rw_near[n].astype(F32)
        ws[...] = w_total.astype(BF16)
        for slot, k in enumerate((2, 1, 3)):
            send(ws.at[k], rw_x.at[slot], S_W_X, R_W_X, along_x(k if k < 3 else -1))
    with jax.named_scope("relay"):
        wait(rz6, recv_sems.at[R_Z6])
        wait(rz54, recv_sems.at[R_Z54])
        z_relay()
    with jax.named_scope("gather0"):
        grad[0, my_rows] = z_total(0).reshape(ROWS, BS).astype(BF16)
        gather(0)
    with jax.named_scope("gather1"):
        grad[1, pl.ds(pl.multiple_of(y * ROWS, ROWS), HALF)] = z_total(1)[0].astype(BF16)
        wait(rw_x, recv_sems.at[R_W_X])
        last = w_total[0]
        for slot in range(3):
            last = last + rw_x[slot].astype(F32)
        grad[1, my_last] = last.astype(BF16)
        gather(1)
    with jax.named_scope("task_wait"):
        wait(task_top.at[:, pl.ds(0, MID - HALF)], recv_sems.at[R_TASK_TOP])
        wait(task_low.at[:, pl.ds(0, MID - HALF)], recv_sems.at[R_TASK_LOW])
    with jax.named_scope("unfold"):
        for t in range(TASKS):
            top = DECAY_RATE * task_top[t].astype(F32)
            task_stats[t, pl.ds(0, MID)] = top
            task_stats[t, right, pl.ds(0, MID)] = top[:, MID:].T
            task_stats[t, right, right] = DECAY_RATE * task_low[t].astype(F32)

    def grams(j):
        block = grad[j]
        gram[2 * j] = dot(block, block, ((1,), (1,)))
        gram[2 * j + 1] = dot(block, block, ((0,), (0,)))

    def precondition(j):
        block = grad[j]
        left = inverse_root(task_stats[2 * j] + gram[2 * j])
        right_root = inverse_root(task_stats[2 * j + 1] + gram[2 * j + 1])
        half = dot(left, block).astype(BF16)
        pre = dot(half, right_root)
        pre_ref[...] = pre
        wide = block.astype(F32)
        scale = jnp.sqrt(jnp.sum(wide * wide) + NORM_EPSILON) / jnp.sqrt(jnp.sum(pre * pre) + NORM_EPSILON)
        upd_rows[j] = (pre_ref[my_rows] * scale).astype(BF16)

    with jax.named_scope("grad_wait0"):
        wait(grad.at[0, pl.ds(0, BS - ROWS)], recv_sems.at[R_GRAD])
    grams(0)
    precondition(0)
    with jax.named_scope("grad_wait1"):
        wait(grad.at[1, pl.ds(0, BS - ROWS)], recv_sems.at[R_GRAD + 1])
    grams(1)
    with jax.named_scope("stats_out"):
        for c in range(CAP):
            matches = [
                jnp.logical_and(owners[t] == y, ranks[t] == c).astype(jnp.int32) for t in range(TASKS)
            ]
            used = sum(matches, jnp.int32(0))
            task = sum((t * matches[t] for t in range(TASKS)), jnp.int32(0))
            fresh = DECAY_RATE * slots_in[c] + gram[jnp.minimum(task, TASKS - 1)]
            new_stats[c] = jnp.where(used > 0, fresh, jnp.zeros_like(fresh))
        stats_copy = pltpu.make_async_copy(new_stats, stats_out, local_sems.at[L_STATS_OUT])
        stats_copy.start()
    precondition(1)
    update_copy = pltpu.make_async_copy(upd_rows, update, local_sems.at[L_UPDATE])
    update_copy.start()
    with jax.named_scope("sent"):
        wait(own, send_sems.at[S_CORE])
        wait(chip.at[pl.ds(0, 3), :, pl.ds(0, X_UNITS)], send_sems.at[S_X])
        wait(rz6, send_sems.at[S_Z6])
        wait(rz54, send_sems.at[S_Z54])
        wait(rz_near0, send_sems.at[S_Z_NEAR])
        wait(rz_near1, send_sems.at[S_Z_NEAR + 1])
        wait(rw6, send_sems.at[S_W6])
        wait(rw54, send_sems.at[S_W54])
        wait(rw_near, send_sems.at[S_W_NEAR])
        wait(rw_x, send_sems.at[S_W_X])
        wait(slot_top.at[pl.ds(0, NY - 1)], send_sems.at[S_SLOT_TOP])
        wait(slot_low.at[pl.ds(0, NY - 1)], send_sems.at[S_SLOT_LOW])
        wait(task_top.at[:, pl.ds(0, MID - HALF)], send_sems.at[S_TASK_TOP])
        wait(task_low.at[:, pl.ds(0, MID - HALF)], send_sems.at[S_TASK_LOW])
        wait(grad.at[:, pl.ds(0, BS - ROWS)], send_sems.at[S_GRAD])
    with jax.named_scope("out"):
        stats_copy.wait()
        update_copy.wait()


def write_out(update_in, stats_in, update, stats_out):
    update[...] = update_in[...]
    stats_out[...] = stats_in[...]


def per_device(grad_parts, stats_in, assignment):
    parts = grad_parts.reshape(NX, NZ, NC, UNITS, HALF, BS)
    slots = stats_in[0]
    assign = assignment.reshape(TASKS)
    any_space = pl.BlockSpec(memory_space=pl.ANY)
    update, stats_out = pl.pallas_call(
        kernel,
        out_shape=(
            jax.ShapeDtypeStruct((BLOCKS, ROWS, BS), BF16),
            jax.ShapeDtypeStruct((CAP, BS, BS), F32),
        ),
        in_specs=[any_space, any_space, any_space],
        out_specs=(any_space, any_space),
        scratch_shapes=[
            pltpu.VMEM((NX, NZ, UNITS, HALF, BS), BF16),
            pltpu.VMEM((NX, NZ, UNITS, HALF, BS), BF16),
            pltpu.VMEM((NX, NZ, UNITS, HALF, BS), BF16),
            pltpu.VMEM((3, FAR, X_UNITS, HALF, BS), BF16),
            pltpu.VMEM((3, NZ - FAR, 2, HALF, BS), BF16),
            pltpu.VMEM((3, NZ - FAR, 1, HALF, BS), BF16),
            pltpu.VMEM((NZ, X_UNITS, HALF, BS), BF16),
            pltpu.VMEM((X_UNITS, HALF, BS), F32),
            pltpu.VMEM((2, X_UNITS, HALF, MID), BF16),
            pltpu.VMEM((2, 2, X_UNITS, HALF, BS), BF16),
            pltpu.VMEM((2, X_UNITS, HALF, BS), BF16),
            pltpu.VMEM((6, 2, HALF, BS), BF16),
            pltpu.VMEM((6, 1, HALF, BS), BF16),
            pltpu.VMEM((2, NX, HALF, MID), BF16),
            pltpu.VMEM((2, 2, NX, HALF, BS), BF16),
            pltpu.VMEM((2, NX, HALF, BS), BF16),
            pltpu.VMEM((6, NX, HALF, BS), BF16),
            pltpu.VMEM((NX, HALF, BS), BF16),
            pltpu.VMEM((3, HALF, BS), BF16),
            pltpu.VMEM((BLOCKS, BS, BS), BF16),
            pltpu.VMEM((CAP, BS, BS), F32),
            pltpu.VMEM((CAP, BS, BS), BF16),
            pltpu.VMEM((NY, CAP, HALF, BS), BF16),
            pltpu.VMEM((NY, CAP, HALF, MID), BF16),
            pltpu.VMEM((TASKS, MID, BS), BF16),
            pltpu.VMEM((TASKS, MID, MID), BF16),
            pltpu.VMEM((TASKS, BS, BS), F32),
            pltpu.VMEM((TASKS, BS, BS), F32),
            pltpu.VMEM((CAP, BS, BS), F32),
            pltpu.VMEM((BS, BS), F32),
            pltpu.VMEM((BLOCKS, ROWS, BS), BF16),
            pltpu.SMEM((TASKS,), jnp.int32),
            pltpu.SemaphoreType.DMA((N_SEND,)),
            pltpu.SemaphoreType.DMA((N_RECV,)),
            pltpu.SemaphoreType.DMA((N_LOCAL,)),
            pltpu.SemaphoreType.REGULAR((N_IN,)),
        ],
        compiler_params=pltpu.CompilerParams(
            collective_id=0, has_side_effects=True, vmem_limit_bytes=60 * 1024 * 1024
        ),
        name="shampoo_step",
    )(parts, slots, assign)
    update, stats_out = pl.pallas_call(
        write_out,
        out_shape=(
            jax.ShapeDtypeStruct((BLOCKS, ROWS, BS), BF16),
            jax.ShapeDtypeStruct((CAP, BS, BS), F32),
        ),
        name="write_out",
    )(update, stats_out)
    return update, stats_out[None]


def solution(mesh):
    in_specs = (P("dp", None, "owner", None), P("dp", "owner", None, None), P("dp", None, None))
    out_specs = (P("dp", "owner", None), P("dp", "owner", None, None))
    return jax.shard_map(
        per_device, mesh=mesh, in_specs=in_specs, out_specs=out_specs, check_vma=False
    )
```

```python
import jax
import jax.numpy as jnp
from jax import lax
from jax.experimental import pallas as pl
from jax.experimental.pallas import tpu as pltpu
from jax.sharding import PartitionSpec as P

NX, NZ, NC, NY = 4, 12, 2, 8
BLOCKS = 2
TASKS = 4
CAP = 2
BS = 256
MID = BS // 2
ROWS = BS // NY
HALF = ROWS // 2
FAR = 5
DECAY_RATE = 0.95
NORM_EPSILON = 1e-06
MESH = pl.DeviceIdType.MESH
F32 = jnp.float32
BF16 = jnp.bfloat16

Z_ORDER = (6, 5, -5, 4, -4, 3, -3, 2, -2, 1, -1, 0)
Y_ORDER = (4, 3, 5, 2, 6, 1, 7)
UNITS = 4
X_UNITS = 3
LAST = UNITS - 1
GROUPS = (pl.ds(0, 2), pl.ds(2, 1))

R_CORE_FAR, R_CORE_NEAR, R_X_FAR, R_X_NEAR, R_Z6, R_Z54, R_Z_NEAR, R_SLOT_TOP, R_SLOT_LOW = 0, 4, 8, 9, 11, 12, 13, 15, 16
R_TASK_TOP, R_TASK_LOW, R_GRAD, R_W6, R_W54, R_W_NEAR, R_W_X = 17, 18, 19, 21, 22, 23, 24
N_RECV = 25
S_CORE, S_X, S_Z6, S_Z54, S_SLOT_TOP, S_SLOT_LOW, S_TASK_TOP, S_TASK_LOW, S_GRAD, S_W6, S_W54, S_W_NEAR, S_W_X = range(13)
S_Z_NEAR = 13
N_SEND = 15
L_OWN_FAR, L_OWN_NEAR, L_STATS, L_STATS_OUT, L_UPDATE, L_ASSIGN = 0, 4, 8, 9, 10, 11
N_LOCAL = 12
IN_X, IN_Y, IN_Z = 0, 1, 4
N_IN = 6


def dot(left, right, dims=((1,), (0,))):
    return lax.dot_general(left, right, (dims, ((), ())), preferred_element_type=F32)


def inverse_root(stats):
    scale = 0.25 * lax.rsqrt(jnp.sum(stats * stats) + NORM_EPSILON)
    first = stats * scale
    first16 = first.astype(BF16)
    second = dot(first16, first16)
    second16 = second.astype(BF16)
    third = dot(first16, second16)
    third16 = third.astype(BF16)
    upper = dot((15.625 * first - 6.25 * second + third).astype(BF16), third16)
    rows = lax.broadcasted_iota(jnp.int32, (BS, BS), 0)
    columns = lax.broadcasted_iota(jnp.int32, (BS, BS), 1)
    diagonal = jnp.where(rows == columns, F32(1.5625), F32(0.0))
    root = diagonal - 4.3017578125 * first + 12.20703125 * second - 19.53125 * third + upper
    return root.astype(BF16)


def kernel(parts, stats_in, assign_in, update, stats_out,
           own, other, chip, rx_far, rx_near0, rx_near1,
           xs, xs_own, rz6, rz54, tx_z, rz_near0, rz_near1, rw6, rw54, tx_w, rw_near, ws, rw_x,
           grad, slots_in, slots16, slot_top, slot_low,
           task_top, task_low, task_stats, gram, new_stats, pre_ref, upd_rows,
           assign, send_sems, recv_sems, local_sems, in_sems):
    dp = lax.axis_index("dp")
    y = lax.axis_index("owner")
    x = dp // (NZ * NC)
    rest = dp - x * (NZ * NC)
    z = rest // NC
    core = rest - z * NC

    def around(position, step, size):
        moved = position + (step if step >= 0 else step + size)
        return moved - size * (moved >= size).astype(jnp.int32)

    x_at = [around(x, k, NX) for k in range(NX)]
    z_at = [around(z, step, NZ) for step in Z_ORDER]
    y_at = [around(y, d, NY) for d in range(NY)]

    def along_x(step):
        return (x_at[step % NX] * (NZ * NC) + rest, y)

    def along_z(step):
        return ((x * NZ + z_at[Z_ORDER.index(step)]) * NC + core, y)

    def along_y(d):
        return (dp, y_at[d])

    sibling = (dp + 1 - 2 * core, y)

    partners = [sibling, along_x(1), along_x(-1), along_z(1), along_z(-1), along_y(1), along_y(NY - 1)]
    barrier = pltpu.get_barrier_semaphore()
    for partner in partners:
        pl.semaphore_signal(barrier, inc=1, device_id=partner, device_id_type=MESH)

    def send(src, dst, send_number, recv_number, target):
        pltpu.make_async_remote_copy(
            src_ref=src, dst_ref=dst, send_sem=send_sems.at[send_number], recv_sem=recv_sems.at[recv_number],
            device_id=target, device_id_type=MESH,
        ).start()

    def wait(ref, sem):
        pltpu.make_async_copy(ref, ref, sem).wait()

    far, near = pl.ds(0, FAR), pl.ds(FAR, NZ - FAR)

    def load_own(k, is_far):
        base = L_OWN_FAR if is_far else L_OWN_NEAR
        for q in range(FAR) if is_far else range(FAR, NZ):
            pltpu.make_async_copy(
                parts.at[x_at[k], z_at[q], core], own.at[k, q], local_sems.at[base + k]
            ).start()

    def send_other(k, is_far):
        base = R_CORE_FAR if is_far else R_CORE_NEAR
        for q in range(FAR) if is_far else range(FAR, NZ):
            send(parts.at[x_at[k], z_at[q], 1 - core], other.at[k, q], S_CORE, base + k, sibling)

    def chip_sum(k, is_far):
        places = far if is_far else near
        wait(own.at[k, places], local_sems.at[(L_OWN_FAR if is_far else L_OWN_NEAR) + k])
        wait(other.at[k, places], recv_sems.at[(R_CORE_FAR if is_far else R_CORE_NEAR) + k])
        chip[k, places] = own[k, places] + other[k, places]

    load_own(2, True)
    stats_load = pltpu.make_async_copy(stats_in, slots_in, local_sems.at[L_STATS])
    stats_load.start()
    assign_load = pltpu.make_async_copy(assign_in, assign, local_sems.at[L_ASSIGN])
    assign_load.start()
    with jax.named_scope("barrier"):
        pl.semaphore_wait(barrier, len(partners))
    in_x = (along_x(1), along_x(-1))
    in_y = (along_y(1), along_y(NY - 1))
    in_z = (along_z(1), along_z(-1))

    def tell(number, neighbours):
        for neighbour in neighbours:
            pl.semaphore_signal(in_sems.at[number], inc=1, device_id=neighbour, device_id_type=MESH)

    def hear(number):
        pl.semaphore_wait(in_sems.at[number], 2)

    tell(IN_X, in_x)
    tell(IN_Y, in_y)
    tell(IN_Z, in_z)
    for k in (2, 1, 3, 0):
        send_other(k, True)
    for k in (1, 3, 0):
        load_own(k, True)
    for k in (2, 1, 3, 0):
        load_own(k, False)

    hear(IN_Y)
    tell(IN_Y + 1, in_y)
    hear(IN_Z)
    tell(IN_Z + 1, in_z)
    for k in (2, 1, 3, 0):
        send_other(k, False)

    with jax.named_scope("chip_far"):
        chip_sum(2, True)
        hear(IN_X)
        send(chip.at[2, far, pl.ds(0, X_UNITS)], rx_far.at[0], S_X, R_X_FAR, along_x(2))
        chip_sum(1, True)
        send(chip.at[1, far, pl.ds(0, X_UNITS)], rx_far.at[1], S_X, R_X_FAR, along_x(1))
        chip_sum(3, True)
        send(chip.at[3, far, pl.ds(0, X_UNITS)], rx_far.at[2], S_X, R_X_FAR, along_x(-1))
        chip_sum(0, True)
    hear(IN_Y + 1)
    tell(IN_Y + 2, in_y)
    hear(IN_Z + 1)
    left, right = pl.ds(0, MID), pl.ds(MID, MID)
    with jax.named_scope("w_far"):
        for side, sign in enumerate((1, -1)):
            send(chip.at[:, 0, LAST, :, (left, right)[side]], rw6.at[side], S_W6, R_W6, along_z(3 * sign))
            send(chip.at[:, 1 + side, LAST], rw54.at[side, 0], S_W54, R_W54, along_z(2 * sign))
            send(chip.at[:, 3 + side, LAST], rw54.at[side, 1], S_W54, R_W54, along_z(sign))
    with jax.named_scope("chip_near"):
        chip_sum(2, False)
        chip_sum(1, False)
        chip_sum(3, False)
        for j, ref in enumerate((rx_near0, rx_near1)):
            for slot, k in enumerate((2, 1, 3)):
                send(chip.at[k, near, GROUPS[j]], ref.at[slot], S_X, R_X_NEAR + j, along_x(k if k < 3 else -1))
        chip_sum(0, False)
        for side, sign in enumerate((1, -1)):
            send(chip.at[:, 7 + side, LAST], rw_near.at[2 + side], S_W_NEAR, R_W_NEAR, along_z(2 * sign))
            send(chip.at[:, 9 + side, LAST], rw_near.at[4 + side], S_W_NEAR, R_W_NEAR, along_z(sign))
    hear(IN_Y + 2)

    my_eighth = pl.ds(pl.multiple_of(y * HALF, HALF), HALF)
    my_low = pl.ds(pl.multiple_of(MID + y * HALF, HALF), HALF)
    with jax.named_scope("slots"):
        stats_load.wait()
        slots16[...] = slots_in[...].astype(BF16)
        for d in Y_ORDER:
            top_rows = pl.ds(pl.multiple_of(y_at[d] * HALF, HALF), HALF)
            low_rows = pl.ds(pl.multiple_of(MID + y_at[d] * HALF, HALF), HALF)
            send(slots16.at[:, top_rows], slot_top.at[y], S_SLOT_TOP, R_SLOT_TOP, along_y(d))
            send(slots16.at[:, low_rows, right], slot_low.at[y], S_SLOT_LOW, R_SLOT_LOW, along_y(d))
        slot_top[y] = slots16[:, my_eighth]
        slot_low[y] = slots16[:, my_low, right]

    with jax.named_scope("z_far"):
        wait(rx_far, recv_sems.at[R_X_FAR])
        total = chip[0, far, pl.ds(0, X_UNITS)].astype(F32)
        for slot in range(3):
            total = total + rx_far[slot].astype(F32)
        xs[far] = total.astype(BF16)
        for side, sign in enumerate((1, -1)):
            send(xs.at[0, :, :, (left, right)[side]], rz6.at[side], S_Z6, R_Z6, along_z(3 * sign))
            send(xs.at[1 + side], rz54.at[side, 0], S_Z54, R_Z54, along_z(2 * sign))
            send(xs.at[3 + side], rz54.at[side, 1], S_Z54, R_Z54, along_z(sign))

    with jax.named_scope("w_relay"):
        wait(rw6, recv_sems.at[R_W6])
        wait(rw54, recv_sems.at[R_W54])
        for side, sign in enumerate((1, -1)):
            total = chip[:, 5 + side, LAST].astype(F32) + rw54[side, 0].astype(F32) + rw54[side, 1].astype(F32)
            part, other_part = (left, right) if side == 0 else (right, left)
            halves = (total[:, :, :MID], total[:, :, MID:])
            tx_w[side, :, :, part] = (halves[side] + rw6[side].astype(F32)).astype(BF16)
            tx_w[side, :, :, other_part] = halves[1 - side].astype(BF16)
            send(tx_w.at[side], rw_near.at[side], S_W_NEAR, R_W_NEAR, along_z(3 * sign))

    assign_load.wait()
    owners = [assign[t] for t in range(TASKS)]
    ranks = [
        sum(((owners[s] == owners[t]).astype(jnp.int32) for s in range(t)), jnp.int32(0)) for t in range(TASKS)
    ]
    with jax.named_scope("tasks"):
        wait(slot_top.at[pl.ds(0, NY - 1)], recv_sems.at[R_SLOT_TOP])
        wait(slot_low.at[pl.ds(0, NY - 1)], recv_sems.at[R_SLOT_LOW])
        for t in range(TASKS):
            rank = jnp.minimum(ranks[t], CAP - 1)
            task_top[t, my_eighth] = slot_top[owners[t], rank]
            task_low[t, my_eighth] = slot_low[owners[t], rank]
        for d in Y_ORDER:
            send(task_top.at[:, my_eighth], task_top.at[:, my_eighth], S_TASK_TOP, R_TASK_TOP, along_y(d))
            send(task_low.at[:, my_eighth], task_low.at[:, my_eighth], S_TASK_LOW, R_TASK_LOW, along_y(d))


    rz_near = (rz_near0, rz_near1)
    rx_near = (rx_near0, rx_near1)

    def z_near(j):
        wait(rx_near[j], recv_sems.at[R_X_NEAR + j])
        total = chip[0, near, GROUPS[j]].astype(F32)
        for slot in range(3):
            total = total + rx_near[j][slot].astype(F32)
        xs[near, GROUPS[j]] = total.astype(BF16)
        xs_own[GROUPS[j]] = total[NZ - FAR - 1]
        for side, sign in enumerate((1, -1)):
            send(xs.at[7 + side, GROUPS[j]], rz_near[j].at[2 + side], S_Z_NEAR + j, R_Z_NEAR + j, along_z(2 * sign))
            send(xs.at[9 + side, GROUPS[j]], rz_near[j].at[4 + side], S_Z_NEAR + j, R_Z_NEAR + j, along_z(sign))

    def z_relay(j):
        units = GROUPS[j]
        for side, sign in enumerate((1, -1)):
            total = xs[5 + side, units].astype(F32)
            total = total + rz54[side, 0, units].astype(F32) + rz54[side, 1, units].astype(F32)
            part, other_part = (left, right) if side == 0 else (right, left)
            halves = (total[:, :, :MID], total[:, :, MID:])
            tx_z[side, units, :, part] = (halves[side] + rz6[side, units].astype(F32)).astype(BF16)
            tx_z[side, units, :, other_part] = halves[1 - side].astype(BF16)
            send(tx_z.at[side, units], rz_near[j].at[side], S_Z_NEAR + j, R_Z_NEAR + j, along_z(3 * sign))

    my_rows = pl.ds(pl.multiple_of(y * ROWS, ROWS), ROWS)
    my_last = pl.ds(pl.multiple_of(y * ROWS + HALF, HALF), HALF)

    def z_total(j):
        wait(rz_near[j], recv_sems.at[R_Z_NEAR + j])
        total = xs_own[GROUPS[j]]
        for n in range(6):
            total = total + rz_near[j][n].astype(F32)
        return total

    def gather(j):
        for d in Y_ORDER:
            send(grad.at[j, my_rows], grad.at[j, my_rows], S_GRAD, R_GRAD + j, along_y(d))

    with jax.named_scope("z_near0"):
        z_near(0)
    with jax.named_scope("relay0"):
        wait(rz6, recv_sems.at[R_Z6])
        wait(rz54, recv_sems.at[R_Z54])
        z_relay(0)
    with jax.named_scope("z_near1"):
        z_near(1)
    with jax.named_scope("relay1"):
        z_relay(1)
    with jax.named_scope("w_x"):
        wait(rw_near, recv_sems.at[R_W_NEAR])
        w_total = chip[:, NZ - 1, LAST].astype(F32)
        for n in range(6):
            w_total = w_total + rw_near[n].astype(F32)
        ws[...] = w_total.astype(BF16)
        for slot, k in enumerate((2, 1, 3)):
            send(ws.at[k], rw_x.at[slot], S_W_X, R_W_X, along_x(k if k < 3 else -1))
    with jax.named_scope("gather0"):
        grad[0, my_rows] = z_total(0).reshape(ROWS, BS).astype(BF16)
        gather(0)
    with jax.named_scope("gather1"):
        grad[1, pl.ds(pl.multiple_of(y * ROWS, ROWS), HALF)] = z_total(1)[0].astype(BF16)
        wait(rw_x, recv_sems.at[R_W_X])
        last = w_total[0]
        for slot in range(3):
            last = last + rw_x[slot].astype(F32)
        grad[1, my_last] = last.astype(BF16)
        gather(1)
    with jax.named_scope("task_wait"):
        wait(task_top.at[:, pl.ds(0, MID - HALF)], recv_sems.at[R_TASK_TOP])
        wait(task_low.at[:, pl.ds(0, MID - HALF)], recv_sems.at[R_TASK_LOW])
    with jax.named_scope("unfold"):
        for t in range(TASKS):
            top = DECAY_RATE * task_top[t].astype(F32)
            task_stats[t, pl.ds(0, MID)] = top
            task_stats[t, right, pl.ds(0, MID)] = top[:, MID:].T
            task_stats[t, right, right] = DECAY_RATE * task_low[t].astype(F32)

    def grams(j):
        block = grad[j]
        gram[2 * j] = dot(block, block, ((1,), (1,)))
        gram[2 * j + 1] = dot(block, block, ((0,), (0,)))

    def precondition(j):
        block = grad[j]
        left = inverse_root(task_stats[2 * j] + gram[2 * j])
        right_root = inverse_root(task_stats[2 * j + 1] + gram[2 * j + 1])
        half = dot(left, block).astype(BF16)
        pre = dot(half, right_root)
        pre_ref[...] = pre
        wide = block.astype(F32)
        scale = jnp.sqrt(jnp.sum(wide * wide) + NORM_EPSILON) / jnp.sqrt(jnp.sum(pre * pre) + NORM_EPSILON)
        upd_rows[j] = (pre_ref[my_rows] * scale).astype(BF16)

    with jax.named_scope("grad_wait0"):
        wait(grad.at[0, pl.ds(0, BS - ROWS)], recv_sems.at[R_GRAD])
    grams(0)
    precondition(0)
    with jax.named_scope("grad_wait1"):
        wait(grad.at[1, pl.ds(0, BS - ROWS)], recv_sems.at[R_GRAD + 1])
    grams(1)
    with jax.named_scope("stats_out"):
        for c in range(CAP):
            matches = [
                jnp.logical_and(owners[t] == y, ranks[t] == c).astype(jnp.int32) for t in range(TASKS)
            ]
            used = sum(matches, jnp.int32(0))
            task = sum((t * matches[t] for t in range(TASKS)), jnp.int32(0))
            fresh = DECAY_RATE * slots_in[c] + gram[jnp.minimum(task, TASKS - 1)]
            new_stats[c] = jnp.where(used > 0, fresh, jnp.zeros_like(fresh))
        stats_copy = pltpu.make_async_copy(new_stats, stats_out, local_sems.at[L_STATS_OUT])
        stats_copy.start()
    precondition(1)
    update_copy = pltpu.make_async_copy(upd_rows, update, local_sems.at[L_UPDATE])
    update_copy.start()
    with jax.named_scope("sent"):
        wait(own, send_sems.at[S_CORE])
        wait(chip.at[pl.ds(0, 3), :, pl.ds(0, X_UNITS)], send_sems.at[S_X])
        wait(rz6, send_sems.at[S_Z6])
        wait(rz54, send_sems.at[S_Z54])
        wait(rz_near0, send_sems.at[S_Z_NEAR])
        wait(rz_near1, send_sems.at[S_Z_NEAR + 1])
        wait(rw6, send_sems.at[S_W6])
        wait(rw54, send_sems.at[S_W54])
        wait(rw_near, send_sems.at[S_W_NEAR])
        wait(rw_x, send_sems.at[S_W_X])
        wait(slot_top.at[pl.ds(0, NY - 1)], send_sems.at[S_SLOT_TOP])
        wait(slot_low.at[pl.ds(0, NY - 1)], send_sems.at[S_SLOT_LOW])
        wait(task_top.at[:, pl.ds(0, MID - HALF)], send_sems.at[S_TASK_TOP])
        wait(task_low.at[:, pl.ds(0, MID - HALF)], send_sems.at[S_TASK_LOW])
        wait(grad.at[:, pl.ds(0, BS - ROWS)], send_sems.at[S_GRAD])
    with jax.named_scope("out"):
        stats_copy.wait()
        update_copy.wait()


def write_out(update_in, stats_in, update, stats_out):
    update[...] = update_in[...]
    stats_out[...] = stats_in[...]


def per_device(grad_parts, stats_in, assignment):
    parts = grad_parts.reshape(NX, NZ, NC, UNITS, HALF, BS)
    slots = stats_in[0]
    assign = assignment.reshape(TASKS)
    any_space = pl.BlockSpec(memory_space=pl.ANY)
    update, stats_out = pl.pallas_call(
        kernel,
        out_shape=(
            jax.ShapeDtypeStruct((BLOCKS, ROWS, BS), BF16),
            jax.ShapeDtypeStruct((CAP, BS, BS), F32),
        ),
        in_specs=[any_space, any_space, any_space],
        out_specs=(any_space, any_space),
        scratch_shapes=[
            pltpu.VMEM((NX, NZ, UNITS, HALF, BS), BF16),
            pltpu.VMEM((NX, NZ, UNITS, HALF, BS), BF16),
            pltpu.VMEM((NX, NZ, UNITS, HALF, BS), BF16),
            pltpu.VMEM((3, FAR, X_UNITS, HALF, BS), BF16),
            pltpu.VMEM((3, NZ - FAR, 2, HALF, BS), BF16),
            pltpu.VMEM((3, NZ - FAR, 1, HALF, BS), BF16),
            pltpu.VMEM((NZ, X_UNITS, HALF, BS), BF16),
            pltpu.VMEM((X_UNITS, HALF, BS), F32),
            pltpu.VMEM((2, X_UNITS, HALF, MID), BF16),
            pltpu.VMEM((2, 2, X_UNITS, HALF, BS), BF16),
            pltpu.VMEM((2, X_UNITS, HALF, BS), BF16),
            pltpu.VMEM((6, 2, HALF, BS), BF16),
            pltpu.VMEM((6, 1, HALF, BS), BF16),
            pltpu.VMEM((2, NX, HALF, MID), BF16),
            pltpu.VMEM((2, 2, NX, HALF, BS), BF16),
            pltpu.VMEM((2, NX, HALF, BS), BF16),
            pltpu.VMEM((6, NX, HALF, BS), BF16),
            pltpu.VMEM((NX, HALF, BS), BF16),
            pltpu.VMEM((3, HALF, BS), BF16),
            pltpu.VMEM((BLOCKS, BS, BS), BF16),
            pltpu.VMEM((CAP, BS, BS), F32),
            pltpu.VMEM((CAP, BS, BS), BF16),
            pltpu.VMEM((NY, CAP, HALF, BS), BF16),
            pltpu.VMEM((NY, CAP, HALF, MID), BF16),
            pltpu.VMEM((TASKS, MID, BS), BF16),
            pltpu.VMEM((TASKS, MID, MID), BF16),
            pltpu.VMEM((TASKS, BS, BS), F32),
            pltpu.VMEM((TASKS, BS, BS), F32),
            pltpu.VMEM((CAP, BS, BS), F32),
            pltpu.VMEM((BS, BS), F32),
            pltpu.VMEM((BLOCKS, ROWS, BS), BF16),
            pltpu.SMEM((TASKS,), jnp.int32),
            pltpu.SemaphoreType.DMA((N_SEND,)),
            pltpu.SemaphoreType.DMA((N_RECV,)),
            pltpu.SemaphoreType.DMA((N_LOCAL,)),
            pltpu.SemaphoreType.REGULAR((N_IN,)),
        ],
        compiler_params=pltpu.CompilerParams(
            collective_id=0, has_side_effects=True, vmem_limit_bytes=60 * 1024 * 1024
        ),
        name="shampoo_step",
    )(parts, slots, assign)
    update, stats_out = pl.pallas_call(
        write_out,
        out_shape=(
            jax.ShapeDtypeStruct((BLOCKS, ROWS, BS), BF16),
            jax.ShapeDtypeStruct((CAP, BS, BS), F32),
        ),
        name="write_out",
    )(update, stats_out)
    return update, stats_out[None]


def solution(mesh):
    in_specs = (P("dp", None, "owner", None), P("dp", "owner", None, None), P("dp", None, None))
    out_specs = (P("dp", "owner", None), P("dp", "owner", None, None))
    return jax.shard_map(
        per_device, mesh=mesh, in_specs=in_specs, out_specs=out_specs, check_vma=False
    )
```

```python
import jax
import jax.numpy as jnp
from jax import lax
from jax.experimental import pallas as pl
from jax.experimental.pallas import tpu as pltpu
from jax.sharding import PartitionSpec as P

NX, NZ, NC, NY = 4, 12, 2, 8
BLOCKS = 2
TASKS = 4
CAP = 2
BS = 256
MID = BS // 2
ROWS = BS // NY
HALF = ROWS // 2
FAR = 5
DECAY_RATE = 0.95
NORM_EPSILON = 1e-06
MESH = pl.DeviceIdType.MESH
F32 = jnp.float32
BF16 = jnp.bfloat16

Z_ORDER = (6, 5, -5, 4, -4, 3, -3, 2, -2, 1, -1, 0)
Y_ORDER = (4, 3, 5, 2, 6, 1, 7)
UNITS = 4
X_UNITS = 3
LAST = UNITS - 1
GROUPS = (pl.ds(0, 2), pl.ds(2, 1))

R_CORE_FAR, R_CORE_NEAR, R_X_FAR, R_X_NEAR, R_Z6, R_Z54, R_Z_NEAR, R_SLOT_TOP, R_SLOT_LOW = 0, 4, 8, 9, 11, 13, 15, 17, 18
R_TASK_TOP, R_TASK_LOW, R_GRAD, R_W6, R_W54, R_W_NEAR, R_W_X = 19, 20, 21, 23, 24, 25, 26
N_RECV = 27
S_CORE, S_X, S_X_FAR, S_SLOT_TOP, S_SLOT_LOW, S_TASK_TOP, S_TASK_LOW, S_GRAD, S_W6, S_W54, S_W_NEAR, S_W_X = range(12)
S_Z6, S_Z54, S_Z_NEAR = 12, 14, 16
N_SEND = 18
L_OWN_FAR, L_OWN_NEAR, L_STATS, L_STATS_OUT, L_UPDATE, L_ASSIGN = 0, 4, 8, 9, 10, 11
N_LOCAL = 12
IN_X, IN_Y, IN_Z = 0, 1, 4
N_IN = 6


def dot(left, right, dims=((1,), (0,))):
    return lax.dot_general(left, right, (dims, ((), ())), preferred_element_type=F32)


def inverse_root(stats):
    scale = 0.25 * lax.rsqrt(jnp.sum(stats * stats) + NORM_EPSILON)
    stats16 = stats.astype(BF16)
    square = dot(stats16, stats16)
    cube = dot(stats16, square.astype(BF16))
    first = stats * scale
    second = square * (scale * scale)
    third = cube * (scale * scale * scale)
    third16 = third.astype(BF16)
    upper = dot((15.625 * first - 6.25 * second + third).astype(BF16), third16)
    rows = lax.broadcasted_iota(jnp.int32, (BS, BS), 0)
    columns = lax.broadcasted_iota(jnp.int32, (BS, BS), 1)
    diagonal = jnp.where(rows == columns, F32(1.5625), F32(0.0))
    root = diagonal - 4.3017578125 * first + 12.20703125 * second - 19.53125 * third + upper
    return root.astype(BF16)


def kernel(parts, stats_in, assign_in, update, stats_out,
           own, other, chip, rx_far, rx_near0, rx_near1,
           xs, xs_own, rz6_0, rz6_1, rz54_0, rz54_1, tx_z, rz_near0, rz_near1, rw6, rw54, tx_w, rw_near, ws, rw_x,
           grad, slots_in, slots16, slot_top, slot_low,
           task_top, task_low, task_stats, gram, new_stats, pre_ref, upd_rows,
           assign, send_sems, recv_sems, local_sems, in_sems):
    dp = lax.axis_index("dp")
    y = lax.axis_index("owner")
    x = dp // (NZ * NC)
    rest = dp - x * (NZ * NC)
    z = rest // NC
    core = rest - z * NC

    def around(position, step, size):
        moved = position + (step if step >= 0 else step + size)
        return moved - size * (moved >= size).astype(jnp.int32)

    x_at = [around(x, k, NX) for k in range(NX)]
    z_at = [around(z, step, NZ) for step in Z_ORDER]
    y_at = [around(y, d, NY) for d in range(NY)]

    def along_x(step):
        return (x_at[step % NX] * (NZ * NC) + rest, y)

    def along_z(step):
        return ((x * NZ + z_at[Z_ORDER.index(step)]) * NC + core, y)

    def along_y(d):
        return (dp, y_at[d])

    sibling = (dp + 1 - 2 * core, y)

    partners = [sibling, along_x(1), along_x(-1), along_z(1), along_z(-1), along_y(1), along_y(NY - 1)]
    barrier = pltpu.get_barrier_semaphore()
    for partner in partners:
        pl.semaphore_signal(barrier, inc=1, device_id=partner, device_id_type=MESH)

    def send(src, dst, send_number, recv_number, target):
        pltpu.make_async_remote_copy(
            src_ref=src, dst_ref=dst, send_sem=send_sems.at[send_number], recv_sem=recv_sems.at[recv_number],
            device_id=target, device_id_type=MESH,
        ).start()

    def wait(ref, sem):
        pltpu.make_async_copy(ref, ref, sem).wait()

    far, near = pl.ds(0, FAR), pl.ds(FAR, NZ - FAR)

    def load_own(k, is_far):
        base = L_OWN_FAR if is_far else L_OWN_NEAR
        for q in range(FAR) if is_far else range(FAR, NZ):
            pltpu.make_async_copy(
                parts.at[x_at[k], z_at[q], core], own.at[k, q], local_sems.at[base + k]
            ).start()

    def send_other(k, is_far):
        base = R_CORE_FAR if is_far else R_CORE_NEAR
        for q in range(FAR) if is_far else range(FAR, NZ):
            send(parts.at[x_at[k], z_at[q], 1 - core], other.at[k, q], S_CORE, base + k, sibling)

    def chip_sum(k, is_far):
        places = far if is_far else near
        wait(own.at[k, places], local_sems.at[(L_OWN_FAR if is_far else L_OWN_NEAR) + k])
        wait(other.at[k, places], recv_sems.at[(R_CORE_FAR if is_far else R_CORE_NEAR) + k])
        chip[k, places] = own[k, places] + other[k, places]

    load_own(2, True)
    stats_load = pltpu.make_async_copy(stats_in, slots_in, local_sems.at[L_STATS])
    stats_load.start()
    assign_load = pltpu.make_async_copy(assign_in, assign, local_sems.at[L_ASSIGN])
    assign_load.start()
    with jax.named_scope("barrier"):
        pl.semaphore_wait(barrier, len(partners))
    in_x = (along_x(1), along_x(-1))
    in_y = (along_y(1), along_y(NY - 1))
    in_z = (along_z(1), along_z(-1))

    def tell(number, neighbours):
        for neighbour in neighbours:
            pl.semaphore_signal(in_sems.at[number], inc=1, device_id=neighbour, device_id_type=MESH)

    def hear(number):
        pl.semaphore_wait(in_sems.at[number], 2)

    tell(IN_X, in_x)
    tell(IN_Y, in_y)
    tell(IN_Z, in_z)
    for k in (2, 1, 3, 0):
        send_other(k, True)
    for k in (1, 3, 0):
        load_own(k, True)
    for k in (2, 1, 3, 0):
        load_own(k, False)
    for k in (2, 1, 3, 0):
        send_other(k, False)

    hear(IN_Y)
    tell(IN_Y + 1, in_y)
    hear(IN_Z)
    tell(IN_Z + 1, in_z)

    with jax.named_scope("chip_far"):
        chip_sum(2, True)
        hear(IN_X)
        send(chip.at[2, far, pl.ds(0, X_UNITS)], rx_far.at[0], S_X_FAR, R_X_FAR, along_x(2))
        chip_sum(1, True)
        send(chip.at[1, far, pl.ds(0, X_UNITS)], rx_far.at[1], S_X_FAR, R_X_FAR, along_x(1))
        chip_sum(3, True)
        send(chip.at[3, far, pl.ds(0, X_UNITS)], rx_far.at[2], S_X_FAR, R_X_FAR, along_x(-1))
        chip_sum(0, True)
    hear(IN_Y + 1)
    tell(IN_Y + 2, in_y)
    hear(IN_Z + 1)
    left, right = pl.ds(0, MID), pl.ds(MID, MID)
    with jax.named_scope("w_far"):
        for side, sign in enumerate((1, -1)):
            send(chip.at[:, 0, LAST, :, (left, right)[side]], rw6.at[side], S_W6, R_W6, along_z(3 * sign))
            send(chip.at[:, 1 + side, LAST], rw54.at[side, 0], S_W54, R_W54, along_z(2 * sign))
            send(chip.at[:, 3 + side, LAST], rw54.at[side, 1], S_W54, R_W54, along_z(sign))
    with jax.named_scope("chip_near"):
        chip_sum(2, False)
        chip_sum(1, False)
        chip_sum(3, False)
        chip_sum(0, False)
        for side, sign in enumerate((1, -1)):
            send(chip.at[:, 7 + side, LAST], rw_near.at[2 + side], S_W_NEAR, R_W_NEAR, along_z(2 * sign))
            send(chip.at[:, 9 + side, LAST], rw_near.at[4 + side], S_W_NEAR, R_W_NEAR, along_z(sign))
    hear(IN_Y + 2)

    my_eighth = pl.ds(pl.multiple_of(y * HALF, HALF), HALF)
    my_low = pl.ds(pl.multiple_of(MID + y * HALF, HALF), HALF)
    with jax.named_scope("slots"):
        stats_load.wait()
        slots16[...] = slots_in[...].astype(BF16)
        for d in Y_ORDER:
            top_rows = pl.ds(pl.multiple_of(y_at[d] * HALF, HALF), HALF)
            low_rows = pl.ds(pl.multiple_of(MID + y_at[d] * HALF, HALF), HALF)
            send(slots16.at[:, top_rows], slot_top.at[y], S_SLOT_TOP, R_SLOT_TOP, along_y(d))
            send(slots16.at[:, low_rows, right], slot_low.at[y], S_SLOT_LOW, R_SLOT_LOW, along_y(d))
        slot_top[y] = slots16[:, my_eighth]
        slot_low[y] = slots16[:, my_low, right]

    with jax.named_scope("x_near"):
        wait(rx_far, send_sems.at[S_X_FAR])
        for j, ref in enumerate((rx_near0, rx_near1)):
            for slot, k in enumerate((2, 1, 3)):
                send(chip.at[k, near, GROUPS[j]], ref.at[slot], S_X, R_X_NEAR + j, along_x(k if k < 3 else -1))

    rz6, rz54 = (rz6_0, rz6_1), (rz54_0, rz54_1)

    with jax.named_scope("z_far"):
        wait(rx_far, recv_sems.at[R_X_FAR])
        total = chip[0, far, pl.ds(0, X_UNITS)].astype(F32)
        for slot in range(3):
            total = total + rx_far[slot].astype(F32)
        xs[far] = total.astype(BF16)

    def send_far(j):
        units = GROUPS[j]
        for side, sign in enumerate((1, -1)):
            send(xs.at[0, units, :, (left, right)[side]], rz6[j].at[side], S_Z6 + j, R_Z6 + j, along_z(3 * sign))
            send(xs.at[1 + side, units], rz54[j].at[side, 0], S_Z54 + j, R_Z54 + j, along_z(2 * sign))
            send(xs.at[3 + side, units], rz54[j].at[side, 1], S_Z54 + j, R_Z54 + j, along_z(sign))

    send_far(0)
    with jax.named_scope("w_relay"):
        wait(rw6, recv_sems.at[R_W6])
        wait(rw54, recv_sems.at[R_W54])
        for side, sign in enumerate((1, -1)):
            total = chip[:, 5 + side, LAST].astype(F32) + rw54[side, 0].astype(F32) + rw54[side, 1].astype(F32)
            part, other_part = (left, right) if side == 0 else (right, left)
            halves = (total[:, :, :MID], total[:, :, MID:])
            tx_w[side, :, :, part] = (halves[side] + rw6[side].astype(F32)).astype(BF16)
            tx_w[side, :, :, other_part] = halves[1 - side].astype(BF16)
            send(tx_w.at[side], rw_near.at[side], S_W_NEAR, R_W_NEAR, along_z(3 * sign))

    send_far(1)

    assign_load.wait()
    owners = [assign[t] for t in range(TASKS)]
    ranks = [
        sum(((owners[s] == owners[t]).astype(jnp.int32) for s in range(t)), jnp.int32(0)) for t in range(TASKS)
    ]
    with jax.named_scope("tasks"):
        wait(slot_top.at[pl.ds(0, NY - 1)], recv_sems.at[R_SLOT_TOP])
        wait(slot_low.at[pl.ds(0, NY - 1)], recv_sems.at[R_SLOT_LOW])
        for t in range(TASKS):
            rank = jnp.minimum(ranks[t], CAP - 1)
            task_top[t, my_eighth] = slot_top[owners[t], rank]
            task_low[t, my_eighth] = slot_low[owners[t], rank]
        for d in Y_ORDER:
            send(task_top.at[:, my_eighth], task_top.at[:, my_eighth], S_TASK_TOP, R_TASK_TOP, along_y(d))
            send(task_low.at[:, my_eighth], task_low.at[:, my_eighth], S_TASK_LOW, R_TASK_LOW, along_y(d))


    rz_near = (rz_near0, rz_near1)
    rx_near = (rx_near0, rx_near1)

    def z_near(j):
        wait(rx_near[j], recv_sems.at[R_X_NEAR + j])
        total = chip[0, near, GROUPS[j]].astype(F32)
        for slot in range(3):
            total = total + rx_near[j][slot].astype(F32)
        xs[near, GROUPS[j]] = total.astype(BF16)
        xs_own[GROUPS[j]] = total[NZ - FAR - 1]
        for side, sign in enumerate((1, -1)):
            send(xs.at[7 + side, GROUPS[j]], rz_near[j].at[2 + side], S_Z_NEAR + j, R_Z_NEAR + j, along_z(2 * sign))
            send(xs.at[9 + side, GROUPS[j]], rz_near[j].at[4 + side], S_Z_NEAR + j, R_Z_NEAR + j, along_z(sign))

    def z_relay(j):
        units = GROUPS[j]
        for side, sign in enumerate((1, -1)):
            total = xs[5 + side, units].astype(F32)
            total = total + rz54[j][side, 0].astype(F32) + rz54[j][side, 1].astype(F32)
            part, other_part = (left, right) if side == 0 else (right, left)
            halves = (total[:, :, :MID], total[:, :, MID:])
            tx_z[side, units, :, part] = (halves[side] + rz6[j][side].astype(F32)).astype(BF16)
            tx_z[side, units, :, other_part] = halves[1 - side].astype(BF16)
            send(tx_z.at[side, units], rz_near[j].at[side], S_Z_NEAR + j, R_Z_NEAR + j, along_z(3 * sign))

    my_rows = pl.ds(pl.multiple_of(y * ROWS, ROWS), ROWS)
    my_last = pl.ds(pl.multiple_of(y * ROWS + HALF, HALF), HALF)

    def z_total(j):
        wait(rz_near[j], recv_sems.at[R_Z_NEAR + j])
        total = xs_own[GROUPS[j]]
        for n in range(6):
            total = total + rz_near[j][n].astype(F32)
        return total

    def gather(j):
        for d in Y_ORDER:
            send(grad.at[j, my_rows], grad.at[j, my_rows], S_GRAD, R_GRAD + j, along_y(d))

    with jax.named_scope("z_near0"):
        z_near(0)
    with jax.named_scope("relay0"):
        wait(rz6[0], recv_sems.at[R_Z6])
        wait(rz54[0], recv_sems.at[R_Z54])
        z_relay(0)
    with jax.named_scope("z_near1"):
        z_near(1)
    with jax.named_scope("relay1"):
        wait(rz6[1], recv_sems.at[R_Z6 + 1])
        wait(rz54[1], recv_sems.at[R_Z54 + 1])
        z_relay(1)
    with jax.named_scope("w_x"):
        wait(rw_near, recv_sems.at[R_W_NEAR])
        w_total = chip[:, NZ - 1, LAST].astype(F32)
        for n in range(6):
            w_total = w_total + rw_near[n].astype(F32)
        ws[...] = w_total.astype(BF16)
        for slot, k in enumerate((2, 1, 3)):
            send(ws.at[k], rw_x.at[slot], S_W_X, R_W_X, along_x(k if k < 3 else -1))
    with jax.named_scope("gather0"):
        grad[0, my_rows] = z_total(0).reshape(ROWS, BS).astype(BF16)
        gather(0)
    with jax.named_scope("gather1"):
        grad[1, pl.ds(pl.multiple_of(y * ROWS, ROWS), HALF)] = z_total(1)[0].astype(BF16)
        wait(rw_x, recv_sems.at[R_W_X])
        last = w_total[0]
        for slot in range(3):
            last = last + rw_x[slot].astype(F32)
        grad[1, my_last] = last.astype(BF16)
        gather(1)
    with jax.named_scope("task_wait"):
        wait(task_top.at[:, pl.ds(0, MID - HALF)], recv_sems.at[R_TASK_TOP])
        wait(task_low.at[:, pl.ds(0, MID - HALF)], recv_sems.at[R_TASK_LOW])
    with jax.named_scope("unfold"):
        for t in range(TASKS):
            top = DECAY_RATE * task_top[t].astype(F32)
            task_stats[t, pl.ds(0, MID)] = top
            task_stats[t, right, pl.ds(0, MID)] = top[:, MID:].T
            task_stats[t, right, right] = DECAY_RATE * task_low[t].astype(F32)

    def grams(j):
        block = grad[j]
        gram[2 * j] = dot(block, block, ((1,), (1,)))
        gram[2 * j + 1] = dot(block, block, ((0,), (0,)))

    def precondition(j):
        block = grad[j]
        left = inverse_root(task_stats[2 * j] + gram[2 * j])
        right_root = inverse_root(task_stats[2 * j + 1] + gram[2 * j + 1])
        half = dot(left, block).astype(BF16)
        pre = dot(half, right_root)
        pre_ref[...] = pre
        wide = block.astype(F32)
        scale = jnp.sqrt(jnp.sum(wide * wide) + NORM_EPSILON) / jnp.sqrt(jnp.sum(pre * pre) + NORM_EPSILON)
        upd_rows[j] = (pre_ref[my_rows] * scale).astype(BF16)

    with jax.named_scope("grad_wait0"):
        wait(grad.at[0, pl.ds(0, BS - ROWS)], recv_sems.at[R_GRAD])
    grams(0)
    precondition(0)
    with jax.named_scope("grad_wait1"):
        wait(grad.at[1, pl.ds(0, BS - ROWS)], recv_sems.at[R_GRAD + 1])
    grams(1)
    with jax.named_scope("stats_out"):
        for c in range(CAP):
            matches = [
                jnp.logical_and(owners[t] == y, ranks[t] == c).astype(jnp.int32) for t in range(TASKS)
            ]
            used = sum(matches, jnp.int32(0))
            task = sum((t * matches[t] for t in range(TASKS)), jnp.int32(0))
            fresh = DECAY_RATE * slots_in[c] + gram[jnp.minimum(task, TASKS - 1)]
            new_stats[c] = jnp.where(used > 0, fresh, jnp.zeros_like(fresh))
        stats_copy = pltpu.make_async_copy(new_stats, stats_out, local_sems.at[L_STATS_OUT])
        stats_copy.start()
    precondition(1)
    update_copy = pltpu.make_async_copy(upd_rows, update, local_sems.at[L_UPDATE])
    update_copy.start()
    with jax.named_scope("sent"):
        wait(own, send_sems.at[S_CORE])
        wait(chip.at[pl.ds(0, 3), near, pl.ds(0, X_UNITS)], send_sems.at[S_X])
        for j in range(BLOCKS):
            wait(rz6[j], send_sems.at[S_Z6 + j])
            wait(rz54[j], send_sems.at[S_Z54 + j])
        wait(rz_near0, send_sems.at[S_Z_NEAR])
        wait(rz_near1, send_sems.at[S_Z_NEAR + 1])
        wait(rw6, send_sems.at[S_W6])
        wait(rw54, send_sems.at[S_W54])
        wait(rw_near, send_sems.at[S_W_NEAR])
        wait(rw_x, send_sems.at[S_W_X])
        wait(slot_top.at[pl.ds(0, NY - 1)], send_sems.at[S_SLOT_TOP])
        wait(slot_low.at[pl.ds(0, NY - 1)], send_sems.at[S_SLOT_LOW])
        wait(task_top.at[:, pl.ds(0, MID - HALF)], send_sems.at[S_TASK_TOP])
        wait(task_low.at[:, pl.ds(0, MID - HALF)], send_sems.at[S_TASK_LOW])
        wait(grad.at[:, pl.ds(0, BS - ROWS)], send_sems.at[S_GRAD])
    with jax.named_scope("out"):
        stats_copy.wait()
        update_copy.wait()


def write_out(update_in, stats_in, update, stats_out):
    update[...] = update_in[...]
    stats_out[...] = stats_in[...]


def per_device(grad_parts, stats_in, assignment):
    parts = grad_parts.reshape(NX, NZ, NC, UNITS, HALF, BS)
    slots = stats_in[0]
    assign = assignment.reshape(TASKS)
    any_space = pl.BlockSpec(memory_space=pl.ANY)
    update, stats_out = pl.pallas_call(
        kernel,
        out_shape=(
            jax.ShapeDtypeStruct((BLOCKS, ROWS, BS), BF16),
            jax.ShapeDtypeStruct((CAP, BS, BS), F32),
        ),
        in_specs=[any_space, any_space, any_space],
        out_specs=(any_space, any_space),
        scratch_shapes=[
            pltpu.VMEM((NX, NZ, UNITS, HALF, BS), BF16),
            pltpu.VMEM((NX, NZ, UNITS, HALF, BS), BF16),
            pltpu.VMEM((NX, NZ, UNITS, HALF, BS), BF16),
            pltpu.VMEM((3, FAR, X_UNITS, HALF, BS), BF16),
            pltpu.VMEM((3, NZ - FAR, 2, HALF, BS), BF16),
            pltpu.VMEM((3, NZ - FAR, 1, HALF, BS), BF16),
            pltpu.VMEM((NZ, X_UNITS, HALF, BS), BF16),
            pltpu.VMEM((X_UNITS, HALF, BS), F32),
            pltpu.VMEM((2, 2, HALF, MID), BF16),
            pltpu.VMEM((2, 1, HALF, MID), BF16),
            pltpu.VMEM((2, 2, 2, HALF, BS), BF16),
            pltpu.VMEM((2, 2, 1, HALF, BS), BF16),
            pltpu.VMEM((2, X_UNITS, HALF, BS), BF16),
            pltpu.VMEM((6, 2, HALF, BS), BF16),
            pltpu.VMEM((6, 1, HALF, BS), BF16),
            pltpu.VMEM((2, NX, HALF, MID), BF16),
            pltpu.VMEM((2, 2, NX, HALF, BS), BF16),
            pltpu.VMEM((2, NX, HALF, BS), BF16),
            pltpu.VMEM((6, NX, HALF, BS), BF16),
            pltpu.VMEM((NX, HALF, BS), BF16),
            pltpu.VMEM((3, HALF, BS), BF16),
            pltpu.VMEM((BLOCKS, BS, BS), BF16),
            pltpu.VMEM((CAP, BS, BS), F32),
            pltpu.VMEM((CAP, BS, BS), BF16),
            pltpu.VMEM((NY, CAP, HALF, BS), BF16),
            pltpu.VMEM((NY, CAP, HALF, MID), BF16),
            pltpu.VMEM((TASKS, MID, BS), BF16),
            pltpu.VMEM((TASKS, MID, MID), BF16),
            pltpu.VMEM((TASKS, BS, BS), F32),
            pltpu.VMEM((TASKS, BS, BS), F32),
            pltpu.VMEM((CAP, BS, BS), F32),
            pltpu.VMEM((BS, BS), F32),
            pltpu.VMEM((BLOCKS, ROWS, BS), BF16),
            pltpu.SMEM((TASKS,), jnp.int32),
            pltpu.SemaphoreType.DMA((N_SEND,)),
            pltpu.SemaphoreType.DMA((N_RECV,)),
            pltpu.SemaphoreType.DMA((N_LOCAL,)),
            pltpu.SemaphoreType.REGULAR((N_IN,)),
        ],
        compiler_params=pltpu.CompilerParams(
            collective_id=0, has_side_effects=True, vmem_limit_bytes=60 * 1024 * 1024
        ),
        name="shampoo_step",
    )(parts, slots, assign)
    update, stats_out = pl.pallas_call(
        write_out,
        out_shape=(
            jax.ShapeDtypeStruct((BLOCKS, ROWS, BS), BF16),
            jax.ShapeDtypeStruct((CAP, BS, BS), F32),
        ),
        name="write_out",
    )(update, stats_out)
    return update, stats_out[None]


def solution(mesh):
    in_specs = (P("dp", None, "owner", None), P("dp", "owner", None, None), P("dp", None, None))
    out_specs = (P("dp", "owner", None), P("dp", "owner", None, None))
    return jax.shard_map(
        per_device, mesh=mesh, in_specs=in_specs, out_specs=out_specs, check_vma=False
    )
```

```python
import jax
import jax.numpy as jnp
from jax import lax
from jax.experimental import pallas as pl
from jax.experimental.pallas import tpu as pltpu
from jax.sharding import PartitionSpec as P

NX, NZ, NC, NY = 4, 12, 2, 8
BLOCKS = 2
TASKS = 4
CAP = 2
BS = 256
MID = BS // 2
ROWS = BS // NY
HALF = ROWS // 2
FAR = 5
DECAY_RATE = 0.95
NORM_EPSILON = 1e-06
MESH = pl.DeviceIdType.MESH
F32 = jnp.float32
BF16 = jnp.bfloat16

Z_ORDER = (6, 5, -5, 4, -4, 3, -3, 2, -2, 1, -1, 0)
Y_ORDER = (4, 3, 5, 2, 6, 1, 7)
UNITS = 4
X_UNITS = 3
LAST = UNITS - 1
GROUPS = (pl.ds(0, 2), pl.ds(2, 1))

R_CORE_FAR, R_CORE_NEAR, R_X_FAR, R_X_NEAR, R_Z6, R_Z54, R_Z_NEAR, R_SLOT_TOP, R_SLOT_LOW = 0, 4, 8, 9, 11, 13, 15, 17, 18
R_TASK_TOP, R_TASK_LOW, R_GRAD, R_W6, R_W54, R_W_NEAR, R_W_X = 19, 20, 21, 23, 24, 25, 26
N_RECV = 27
S_CORE, S_X, S_X_FAR, S_SLOT_TOP, S_SLOT_LOW, S_TASK_TOP, S_TASK_LOW, S_GRAD, S_W6, S_W54, S_W_NEAR, S_W_X = range(12)
S_Z6, S_Z54, S_Z_NEAR = 12, 14, 16
N_SEND = 18
L_OWN_FAR, L_OWN_NEAR, L_STATS, L_STATS_OUT, L_UPDATE, L_ASSIGN = 0, 4, 8, 9, 10, 11
N_LOCAL = 12
IN_X, IN_Y, IN_Z = 0, 1, 4
N_IN = 6


def dot(left, right, dims=((1,), (0,))):
    return lax.dot_general(left, right, (dims, ((), ())), preferred_element_type=F32)


def inverse_root(stats):
    scale = 0.25 * lax.rsqrt(jnp.sum(stats * stats) + NORM_EPSILON)
    stats16 = stats.astype(BF16)
    square = dot(stats16, stats16)
    cube = dot(stats16, square.astype(BF16))
    first = stats * scale
    second = square * (scale * scale)
    third = cube * (scale * scale * scale)
    third16 = third.astype(BF16)
    upper = dot((15.625 * first - 6.25 * second + third).astype(BF16), third16)
    rows = lax.broadcasted_iota(jnp.int32, (BS, BS), 0)
    columns = lax.broadcasted_iota(jnp.int32, (BS, BS), 1)
    diagonal = jnp.where(rows == columns, F32(1.5625), F32(0.0))
    root = diagonal - 4.3017578125 * first + 12.20703125 * second - 19.53125 * third + upper
    return root.astype(BF16)


def kernel(parts, stats_in, assign_in, update, stats_out,
           own, other, chip, rx_far, rx_near0, rx_near1,
           xs, xs_own, rz6_0, rz6_1, rz54_0, rz54_1, tx_z, rz_near0, rz_near1, rw6, rw54, tx_w, rw_near, ws, rw_x,
           grad, slots_in, slots16, slot_top, slot_low,
           task_top, task_low, task_stats, gram, new_stats, pre_ref, upd_rows,
           assign, send_sems, recv_sems, local_sems, in_sems):
    dp = lax.axis_index("dp")
    y = lax.axis_index("owner")
    x = dp // (NZ * NC)
    rest = dp - x * (NZ * NC)
    z = rest // NC
    core = rest - z * NC

    def around(position, step, size):
        moved = position + (step if step >= 0 else step + size)
        return moved - size * (moved >= size).astype(jnp.int32)

    x_at = [around(x, k, NX) for k in range(NX)]
    z_at = [around(z, step, NZ) for step in Z_ORDER]
    y_at = [around(y, d, NY) for d in range(NY)]

    def along_x(step):
        return (x_at[step % NX] * (NZ * NC) + rest, y)

    def along_z(step):
        return ((x * NZ + z_at[Z_ORDER.index(step)]) * NC + core, y)

    def along_y(d):
        return (dp, y_at[d])

    sibling = (dp + 1 - 2 * core, y)

    partners = [sibling, along_x(1), along_x(-1), along_z(1), along_z(-1), along_y(1), along_y(NY - 1)]
    barrier = pltpu.get_barrier_semaphore()
    for partner in partners:
        pl.semaphore_signal(barrier, inc=1, device_id=partner, device_id_type=MESH)

    def send(src, dst, send_number, recv_number, target):
        pltpu.make_async_remote_copy(
            src_ref=src, dst_ref=dst, send_sem=send_sems.at[send_number], recv_sem=recv_sems.at[recv_number],
            device_id=target, device_id_type=MESH,
        ).start()

    def wait(ref, sem):
        pltpu.make_async_copy(ref, ref, sem).wait()

    far, near = pl.ds(0, FAR), pl.ds(FAR, NZ - FAR)

    def load_own(k, is_far):
        base = L_OWN_FAR if is_far else L_OWN_NEAR
        for q in range(FAR) if is_far else range(FAR, NZ):
            pltpu.make_async_copy(
                parts.at[x_at[k], z_at[q], core], own.at[k, q], local_sems.at[base + k]
            ).start()

    def send_other(k, is_far):
        base = R_CORE_FAR if is_far else R_CORE_NEAR
        for q in range(FAR) if is_far else range(FAR, NZ):
            send(parts.at[x_at[k], z_at[q], 1 - core], other.at[k, q], S_CORE, base + k, sibling)

    def chip_sum(k, is_far):
        places = far if is_far else near
        wait(own.at[k, places], local_sems.at[(L_OWN_FAR if is_far else L_OWN_NEAR) + k])
        wait(other.at[k, places], recv_sems.at[(R_CORE_FAR if is_far else R_CORE_NEAR) + k])
        chip[k, places] = own[k, places] + other[k, places]

    load_own(2, True)
    stats_load = pltpu.make_async_copy(stats_in, slots_in, local_sems.at[L_STATS])
    stats_load.start()
    assign_load = pltpu.make_async_copy(assign_in, assign, local_sems.at[L_ASSIGN])
    assign_load.start()
    with jax.named_scope("barrier"):
        pl.semaphore_wait(barrier, len(partners))
    in_x = (along_x(1), along_x(-1))
    in_y = (along_y(1), along_y(NY - 1))
    in_z = (along_z(1), along_z(-1))

    def tell(number, neighbours):
        for neighbour in neighbours:
            pl.semaphore_signal(in_sems.at[number], inc=1, device_id=neighbour, device_id_type=MESH)

    def hear(number):
        pl.semaphore_wait(in_sems.at[number], 2)

    tell(IN_X, in_x)
    tell(IN_Y, in_y)
    tell(IN_Z, in_z)
    for k in (2, 1, 3, 0):
        send_other(k, True)
    for k in (1, 3, 0):
        load_own(k, True)
    for k in (2, 1, 3, 0):
        load_own(k, False)
    for k in (2, 1, 3, 0):
        send_other(k, False)

    hear(IN_Y)
    tell(IN_Y + 1, in_y)
    hear(IN_Z)
    tell(IN_Z + 1, in_z)

    with jax.named_scope("chip_far"):
        chip_sum(2, True)
        hear(IN_X)
        send(chip.at[2, far, pl.ds(0, X_UNITS)], rx_far.at[0], S_X_FAR, R_X_FAR, along_x(2))
        chip_sum(1, True)
        send(chip.at[1, far, pl.ds(0, X_UNITS)], rx_far.at[1], S_X_FAR, R_X_FAR, along_x(1))
        chip_sum(3, True)
        send(chip.at[3, far, pl.ds(0, X_UNITS)], rx_far.at[2], S_X_FAR, R_X_FAR, along_x(-1))
        chip_sum(0, True)
    hear(IN_Y + 1)
    tell(IN_Y + 2, in_y)
    hear(IN_Z + 1)
    left, right = pl.ds(0, MID), pl.ds(MID, MID)
    with jax.named_scope("w_far"):
        for side, sign in enumerate((1, -1)):
            send(chip.at[:, 0, LAST, :, (left, right)[side]], rw6.at[side], S_W6, R_W6, along_z(3 * sign))
            send(chip.at[:, 1 + side, LAST], rw54.at[side, 0], S_W54, R_W54, along_z(2 * sign))
            send(chip.at[:, 3 + side, LAST], rw54.at[side, 1], S_W54, R_W54, along_z(sign))
    with jax.named_scope("chip_near"):
        chip_sum(2, False)
        chip_sum(1, False)
        chip_sum(3, False)
        chip_sum(0, False)
        for side, sign in enumerate((1, -1)):
            send(chip.at[:, 7 + side, LAST], rw_near.at[2 + side], S_W_NEAR, R_W_NEAR, along_z(2 * sign))
            send(chip.at[:, 9 + side, LAST], rw_near.at[4 + side], S_W_NEAR, R_W_NEAR, along_z(sign))
    hear(IN_Y + 2)

    my_eighth = pl.ds(pl.multiple_of(y * HALF, HALF), HALF)
    my_low = pl.ds(pl.multiple_of(MID + y * HALF, HALF), HALF)
    with jax.named_scope("slots"):
        stats_load.wait()
        slots16[...] = slots_in[...].astype(BF16)
        for d in Y_ORDER:
            top_rows = pl.ds(pl.multiple_of(y_at[d] * HALF, HALF), HALF)
            low_rows = pl.ds(pl.multiple_of(MID + y_at[d] * HALF, HALF), HALF)
            send(slots16.at[:, top_rows], slot_top.at[y], S_SLOT_TOP, R_SLOT_TOP, along_y(d))
            send(slots16.at[:, low_rows, right], slot_low.at[y], S_SLOT_LOW, R_SLOT_LOW, along_y(d))
        slot_top[y] = slots16[:, my_eighth]
        slot_low[y] = slots16[:, my_low, right]

    with jax.named_scope("x_near"):
        wait(rx_far, send_sems.at[S_X_FAR])
        for j, ref in enumerate((rx_near0, rx_near1)):
            for slot, k in enumerate((2, 1, 3)):
                send(chip.at[k, near, GROUPS[j]], ref.at[slot], S_X, R_X_NEAR + j, along_x(k if k < 3 else -1))

    rz6, rz54 = (rz6_0, rz6_1), (rz54_0, rz54_1)

    with jax.named_scope("z_far"):
        wait(rx_far, recv_sems.at[R_X_FAR])
        total = chip[0, far, pl.ds(0, X_UNITS)].astype(F32)
        for slot in range(3):
            total = total + rx_far[slot].astype(F32)
        xs[far] = total.astype(BF16)

    def send_far(j):
        units = GROUPS[j]
        for side, sign in enumerate((1, -1)):
            send(xs.at[0, units, :, (left, right)[side]], rz6[j].at[side], S_Z6 + j, R_Z6 + j, along_z(3 * sign))
            send(xs.at[1 + side, units], rz54[j].at[side, 0], S_Z54 + j, R_Z54 + j, along_z(2 * sign))
            send(xs.at[3 + side, units], rz54[j].at[side, 1], S_Z54 + j, R_Z54 + j, along_z(sign))

    send_far(0)
    with jax.named_scope("w_relay"):
        wait(rw6, recv_sems.at[R_W6])
        wait(rw54, recv_sems.at[R_W54])
        for side, sign in enumerate((1, -1)):
            total = chip[:, 5 + side, LAST].astype(F32) + rw54[side, 0].astype(F32) + rw54[side, 1].astype(F32)
            part, other_part = (left, right) if side == 0 else (right, left)
            halves = (total[:, :, :MID], total[:, :, MID:])
            tx_w[side, :, :, part] = (halves[side] + rw6[side].astype(F32)).astype(BF16)
            tx_w[side, :, :, other_part] = halves[1 - side].astype(BF16)
            send(tx_w.at[side], rw_near.at[side], S_W_NEAR, R_W_NEAR, along_z(3 * sign))

    send_far(1)

    assign_load.wait()
    owners = [assign[t] for t in range(TASKS)]
    ranks = [
        sum(((owners[s] == owners[t]).astype(jnp.int32) for s in range(t)), jnp.int32(0)) for t in range(TASKS)
    ]
    with jax.named_scope("tasks"):
        wait(slot_top.at[pl.ds(0, NY - 1)], recv_sems.at[R_SLOT_TOP])
        wait(slot_low.at[pl.ds(0, NY - 1)], recv_sems.at[R_SLOT_LOW])
        for t in range(TASKS):
            rank = jnp.minimum(ranks[t], CAP - 1)
            task_top[t, my_eighth] = slot_top[owners[t], rank]
            task_low[t, my_eighth] = slot_low[owners[t], rank]
        for d in Y_ORDER:
            send(task_top.at[:, my_eighth], task_top.at[:, my_eighth], S_TASK_TOP, R_TASK_TOP, along_y(d))
            send(task_low.at[:, my_eighth], task_low.at[:, my_eighth], S_TASK_LOW, R_TASK_LOW, along_y(d))


    rz_near = (rz_near0, rz_near1)
    rx_near = (rx_near0, rx_near1)

    def z_near(j):
        wait(rx_near[j], recv_sems.at[R_X_NEAR + j])
        total = chip[0, near, GROUPS[j]].astype(F32)
        for slot in range(3):
            total = total + rx_near[j][slot].astype(F32)
        xs[near, GROUPS[j]] = total.astype(BF16)
        xs_own[GROUPS[j]] = total[NZ - FAR - 1]
        for side, sign in enumerate((1, -1)):
            send(xs.at[7 + side, GROUPS[j]], rz_near[j].at[2 + side], S_Z_NEAR + j, R_Z_NEAR + j, along_z(2 * sign))
            send(xs.at[9 + side, GROUPS[j]], rz_near[j].at[4 + side], S_Z_NEAR + j, R_Z_NEAR + j, along_z(sign))

    def z_relay(j):
        units = GROUPS[j]
        for side, sign in enumerate((1, -1)):
            total = xs[5 + side, units].astype(F32)
            total = total + rz54[j][side, 0].astype(F32) + rz54[j][side, 1].astype(F32)
            part, other_part = (left, right) if side == 0 else (right, left)
            halves = (total[:, :, :MID], total[:, :, MID:])
            tx_z[side, units, :, part] = (halves[side] + rz6[j][side].astype(F32)).astype(BF16)
            tx_z[side, units, :, other_part] = halves[1 - side].astype(BF16)
            send(tx_z.at[side, units], rz_near[j].at[side], S_Z_NEAR + j, R_Z_NEAR + j, along_z(3 * sign))

    my_rows = pl.ds(pl.multiple_of(y * ROWS, ROWS), ROWS)
    my_last = pl.ds(pl.multiple_of(y * ROWS + HALF, HALF), HALF)

    def z_total(j):
        wait(rz_near[j], recv_sems.at[R_Z_NEAR + j])
        total = xs_own[GROUPS[j]]
        for n in range(6):
            total = total + rz_near[j][n].astype(F32)
        return total

    def gather(j):
        for d in Y_ORDER:
            send(grad.at[j, my_rows], grad.at[j, my_rows], S_GRAD, R_GRAD + j, along_y(d))

    with jax.named_scope("z_near0"):
        z_near(0)
    with jax.named_scope("relay0"):
        wait(rz6[0], recv_sems.at[R_Z6])
        wait(rz54[0], recv_sems.at[R_Z54])
        z_relay(0)
    with jax.named_scope("z_near1"):
        z_near(1)
    with jax.named_scope("relay1"):
        wait(rz6[1], recv_sems.at[R_Z6 + 1])
        wait(rz54[1], recv_sems.at[R_Z54 + 1])
        z_relay(1)
    with jax.named_scope("w_x"):
        wait(rw_near, recv_sems.at[R_W_NEAR])
        w_total = chip[:, NZ - 1, LAST].astype(F32)
        for n in range(6):
            w_total = w_total + rw_near[n].astype(F32)
        ws[...] = w_total.astype(BF16)
        for slot, k in enumerate((2, 1, 3)):
            send(ws.at[k], rw_x.at[slot], S_W_X, R_W_X, along_x(k if k < 3 else -1))
    with jax.named_scope("gather0"):
        grad[0, my_rows] = z_total(0).reshape(ROWS, BS).astype(BF16)
        gather(0)
    with jax.named_scope("gather1"):
        grad[1, pl.ds(pl.multiple_of(y * ROWS, ROWS), HALF)] = z_total(1)[0].astype(BF16)
        wait(rw_x, recv_sems.at[R_W_X])
        last = w_total[0]
        for slot in range(3):
            last = last + rw_x[slot].astype(F32)
        grad[1, my_last] = last.astype(BF16)
        gather(1)
    with jax.named_scope("task_wait"):
        wait(task_top.at[:, pl.ds(0, MID - HALF)], recv_sems.at[R_TASK_TOP])
        wait(task_low.at[:, pl.ds(0, MID - HALF)], recv_sems.at[R_TASK_LOW])
    with jax.named_scope("unfold"):
        for t in range(TASKS):
            top = DECAY_RATE * task_top[t].astype(F32)
            task_stats[t, pl.ds(0, MID)] = top
            task_stats[t, right, pl.ds(0, MID)] = top[:, MID:].T
            task_stats[t, right, right] = DECAY_RATE * task_low[t].astype(F32)

    def grams(j):
        block = grad[j]
        gram[2 * j] = dot(block, block, ((1,), (1,)))
        gram[2 * j + 1] = dot(block, block, ((0,), (0,)))

    def precondition(j):
        block = grad[j]
        left = inverse_root(task_stats[2 * j] + gram[2 * j])
        right_root = inverse_root(task_stats[2 * j + 1] + gram[2 * j + 1])
        half = dot(left, block).astype(BF16)
        pre = dot(half, right_root)
        pre_ref[...] = pre
        wide = block.astype(F32)
        scale = jnp.sqrt(jnp.sum(wide * wide) + NORM_EPSILON) / jnp.sqrt(jnp.sum(pre * pre) + NORM_EPSILON)
        upd_rows[j] = (pre_ref[my_rows] * scale).astype(BF16)

    with jax.named_scope("grad_wait0"):
        wait(grad.at[0, pl.ds(0, BS - ROWS)], recv_sems.at[R_GRAD])
    grams(0)
    precondition(0)
    with jax.named_scope("grad_wait1"):
        wait(grad.at[1, pl.ds(0, BS - ROWS)], recv_sems.at[R_GRAD + 1])
    grams(1)
    with jax.named_scope("stats_out"):
        for c in range(CAP):
            matches = [
                jnp.logical_and(owners[t] == y, ranks[t] == c).astype(jnp.int32) for t in range(TASKS)
            ]
            used = sum(matches, jnp.int32(0))
            task = sum((t * matches[t] for t in range(TASKS)), jnp.int32(0))
            fresh = DECAY_RATE * slots_in[c] + gram[jnp.minimum(task, TASKS - 1)]
            new_stats[c] = jnp.where(used > 0, fresh, jnp.zeros_like(fresh))
        stats_copy = pltpu.make_async_copy(new_stats, stats_out, local_sems.at[L_STATS_OUT])
        stats_copy.start()
    precondition(1)
    update_copy = pltpu.make_async_copy(upd_rows, update, local_sems.at[L_UPDATE])
    update_copy.start()
    with jax.named_scope("sent"):
        wait(own, send_sems.at[S_CORE])
        wait(chip.at[pl.ds(0, 3), near, pl.ds(0, X_UNITS)], send_sems.at[S_X])
        for j in range(BLOCKS):
            wait(rz6[j], send_sems.at[S_Z6 + j])
            wait(rz54[j], send_sems.at[S_Z54 + j])
        wait(rz_near0, send_sems.at[S_Z_NEAR])
        wait(rz_near1, send_sems.at[S_Z_NEAR + 1])
        wait(rw6, send_sems.at[S_W6])
        wait(rw54, send_sems.at[S_W54])
        wait(rw_near, send_sems.at[S_W_NEAR])
        wait(rw_x, send_sems.at[S_W_X])
        wait(slot_top.at[pl.ds(0, NY - 1)], send_sems.at[S_SLOT_TOP])
        wait(slot_low.at[pl.ds(0, NY - 1)], send_sems.at[S_SLOT_LOW])
        wait(task_top.at[:, pl.ds(0, MID - HALF)], send_sems.at[S_TASK_TOP])
        wait(task_low.at[:, pl.ds(0, MID - HALF)], send_sems.at[S_TASK_LOW])
        wait(grad.at[:, pl.ds(0, BS - ROWS)], send_sems.at[S_GRAD])
    with jax.named_scope("out"):
        stats_copy.wait()
        update_copy.wait()


def write_out(update_in, stats_in, update, stats_out, sems):
    copies = [
        pltpu.make_async_copy(stats_in, stats_out, sems.at[0]),
        pltpu.make_async_copy(update_in, update, sems.at[1]),
    ]
    for copy in copies:
        copy.start()
    for copy in copies:
        copy.wait()


def per_device(grad_parts, stats_in, assignment):
    parts = grad_parts.reshape(NX, NZ, NC, UNITS, HALF, BS)
    slots = stats_in[0]
    assign = assignment.reshape(TASKS)
    any_space = pl.BlockSpec(memory_space=pl.ANY)
    update, stats_out = pl.pallas_call(
        kernel,
        out_shape=(
            jax.ShapeDtypeStruct((BLOCKS, ROWS, BS), BF16),
            jax.ShapeDtypeStruct((CAP, BS, BS), F32),
        ),
        in_specs=[any_space, any_space, any_space],
        out_specs=(any_space, any_space),
        scratch_shapes=[
            pltpu.VMEM((NX, NZ, UNITS, HALF, BS), BF16),
            pltpu.VMEM((NX, NZ, UNITS, HALF, BS), BF16),
            pltpu.VMEM((NX, NZ, UNITS, HALF, BS), BF16),
            pltpu.VMEM((3, FAR, X_UNITS, HALF, BS), BF16),
            pltpu.VMEM((3, NZ - FAR, 2, HALF, BS), BF16),
            pltpu.VMEM((3, NZ - FAR, 1, HALF, BS), BF16),
            pltpu.VMEM((NZ, X_UNITS, HALF, BS), BF16),
            pltpu.VMEM((X_UNITS, HALF, BS), F32),
            pltpu.VMEM((2, 2, HALF, MID), BF16),
            pltpu.VMEM((2, 1, HALF, MID), BF16),
            pltpu.VMEM((2, 2, 2, HALF, BS), BF16),
            pltpu.VMEM((2, 2, 1, HALF, BS), BF16),
            pltpu.VMEM((2, X_UNITS, HALF, BS), BF16),
            pltpu.VMEM((6, 2, HALF, BS), BF16),
            pltpu.VMEM((6, 1, HALF, BS), BF16),
            pltpu.VMEM((2, NX, HALF, MID), BF16),
            pltpu.VMEM((2, 2, NX, HALF, BS), BF16),
            pltpu.VMEM((2, NX, HALF, BS), BF16),
            pltpu.VMEM((6, NX, HALF, BS), BF16),
            pltpu.VMEM((NX, HALF, BS), BF16),
            pltpu.VMEM((3, HALF, BS), BF16),
            pltpu.VMEM((BLOCKS, BS, BS), BF16),
            pltpu.VMEM((CAP, BS, BS), F32),
            pltpu.VMEM((CAP, BS, BS), BF16),
            pltpu.VMEM((NY, CAP, HALF, BS), BF16),
            pltpu.VMEM((NY, CAP, HALF, MID), BF16),
            pltpu.VMEM((TASKS, MID, BS), BF16),
            pltpu.VMEM((TASKS, MID, MID), BF16),
            pltpu.VMEM((TASKS, BS, BS), F32),
            pltpu.VMEM((TASKS, BS, BS), F32),
            pltpu.VMEM((CAP, BS, BS), F32),
            pltpu.VMEM((BS, BS), F32),
            pltpu.VMEM((BLOCKS, ROWS, BS), BF16),
            pltpu.SMEM((TASKS,), jnp.int32),
            pltpu.SemaphoreType.DMA((N_SEND,)),
            pltpu.SemaphoreType.DMA((N_RECV,)),
            pltpu.SemaphoreType.DMA((N_LOCAL,)),
            pltpu.SemaphoreType.REGULAR((N_IN,)),
        ],
        compiler_params=pltpu.CompilerParams(
            collective_id=0, has_side_effects=True, vmem_limit_bytes=53 * 1024 * 1024
        ),
        name="shampoo_step",
    )(parts, slots, assign)
    update, stats_out = pl.pallas_call(
        write_out,
        out_shape=(
            jax.ShapeDtypeStruct((BLOCKS, ROWS, BS), BF16),
            jax.ShapeDtypeStruct((CAP, BS, BS), F32),
        ),
        in_specs=[any_space, any_space],
        out_specs=(any_space, any_space),
        scratch_shapes=[pltpu.SemaphoreType.DMA((2,))],
        compiler_params=pltpu.CompilerParams(vmem_limit_bytes=1024 * 1024),
        name="write_out",
    )(update, stats_out)
    return update, stats_out[None]


def solution(mesh):
    in_specs = (P("dp", None, "owner", None), P("dp", "owner", None, None), P("dp", None, None))
    out_specs = (P("dp", "owner", None), P("dp", "owner", None, None))
    return jax.shard_map(
        per_device, mesh=mesh, in_specs=in_specs, out_specs=out_specs, check_vma=False
    )
```

```python
import jax
import jax.numpy as jnp
from jax import lax
from jax.experimental import pallas as pl
from jax.experimental.pallas import tpu as pltpu
from jax.sharding import PartitionSpec as P

NX, NZ, NC, NY = 4, 12, 2, 8
BLOCKS = 2
TASKS = 4
CAP = 2
BS = 256
MID = BS // 2
ROWS = BS // NY
HALF = ROWS // 2
FAR = 5
DECAY_RATE = 0.95
NORM_EPSILON = 1e-06
MESH = pl.DeviceIdType.MESH
F32 = jnp.float32
BF16 = jnp.bfloat16

Z_ORDER = (6, 5, -5, 4, -4, 3, -3, 2, -2, 1, -1, 0)
Y_ORDER = (4, 3, 5, 2, 6, 1, 7)
UNITS = 4
X_UNITS = 3
LAST = UNITS - 1
GROUPS = (pl.ds(0, 2), pl.ds(2, 1))

R_CORE_FAR, R_CORE_NEAR, R_X_FAR, R_X_NEAR, R_Z6, R_Z54, R_Z_NEAR, R_SLOT_TOP, R_SLOT_LOW = 0, 4, 8, 9, 11, 13, 15, 17, 18
R_TASK_TOP, R_TASK_LOW, R_GRAD, R_W6, R_W54, R_W_NEAR, R_W_X = 19, 20, 21, 23, 24, 25, 26
N_RECV = 27
S_CORE, S_X, S_X_FAR, S_SLOT_TOP, S_SLOT_LOW, S_TASK_TOP, S_TASK_LOW, S_GRAD, S_W6, S_W54, S_W_NEAR, S_W_X = range(12)
S_Z6, S_Z54, S_Z_NEAR = 12, 14, 16
N_SEND = 18
L_OWN_FAR, L_OWN_NEAR, L_STATS, L_STATS_OUT, L_UPDATE, L_ASSIGN = 0, 4, 8, 9, 10, 11
N_LOCAL = 12
IN_X, IN_Y, IN_Z = 0, 1, 4
N_IN = 6


def dot(left, right, dims=((1,), (0,))):
    return lax.dot_general(left, right, (dims, ((), ())), preferred_element_type=F32)


def inverse_root(stats):
    scale = 0.25 * lax.rsqrt(jnp.sum(stats * stats) + NORM_EPSILON)
    stats16 = stats.astype(BF16)
    square = dot(stats16, stats16)
    cube = dot(stats16, square.astype(BF16))
    first = stats * scale
    second = square * (scale * scale)
    third = cube * (scale * scale * scale)
    third16 = third.astype(BF16)
    upper = dot((15.625 * first - 6.25 * second + third).astype(BF16), third16)
    rows = lax.broadcasted_iota(jnp.int32, (BS, BS), 0)
    columns = lax.broadcasted_iota(jnp.int32, (BS, BS), 1)
    diagonal = jnp.where(rows == columns, F32(1.5625), F32(0.0))
    root = diagonal - 4.3017578125 * first + 12.20703125 * second - 19.53125 * third + upper
    return root.astype(BF16)


def kernel(parts, stats_in, assign_in, update, stats_out,
           own, other, chip, rx_far, rx_near0, rx_near1,
           xs, xs_own, rz6_0, rz6_1, rz54_0, rz54_1, tx_z, rz_near0, rz_near1, rw6, rw54, tx_w, rw_near, ws, rw_x,
           grad, slots_in, slots16, slot_top, slot_low,
           task_top, task_low, task_stats, gram, new_stats, pre_ref, upd_rows,
           assign, send_sems, recv_sems, local_sems, in_sems):
    dp = lax.axis_index("dp")
    y = lax.axis_index("owner")
    x = dp // (NZ * NC)
    rest = dp - x * (NZ * NC)
    z = rest // NC
    core = rest - z * NC

    def around(position, step, size):
        moved = position + (step if step >= 0 else step + size)
        return moved - size * (moved >= size).astype(jnp.int32)

    x_at = [around(x, k, NX) for k in range(NX)]
    z_at = [around(z, step, NZ) for step in Z_ORDER]
    y_at = [around(y, d, NY) for d in range(NY)]

    def along_x(step):
        return (x_at[step % NX] * (NZ * NC) + rest, y)

    def along_z(step):
        return ((x * NZ + z_at[Z_ORDER.index(step)]) * NC + core, y)

    def along_y(d):
        return (dp, y_at[d])

    sibling = (dp + 1 - 2 * core, y)

    partners = [sibling, along_x(1), along_x(-1), along_z(1), along_z(-1), along_y(1), along_y(NY - 1)]
    barrier = pltpu.get_barrier_semaphore()
    for partner in partners:
        pl.semaphore_signal(barrier, inc=1, device_id=partner, device_id_type=MESH)

    def send(src, dst, send_number, recv_number, target):
        pltpu.make_async_remote_copy(
            src_ref=src, dst_ref=dst, send_sem=send_sems.at[send_number], recv_sem=recv_sems.at[recv_number],
            device_id=target, device_id_type=MESH,
        ).start()

    def wait(ref, sem):
        pltpu.make_async_copy(ref, ref, sem).wait()

    far, near = pl.ds(0, FAR), pl.ds(FAR, NZ - FAR)

    def load_own(k, is_far):
        base = L_OWN_FAR if is_far else L_OWN_NEAR
        for q in range(FAR) if is_far else range(FAR, NZ):
            pltpu.make_async_copy(
                parts.at[x_at[k], z_at[q], core], own.at[k, q], local_sems.at[base + k]
            ).start()

    def send_other(k, is_far):
        base = R_CORE_FAR if is_far else R_CORE_NEAR
        for q in range(FAR) if is_far else range(FAR, NZ):
            send(parts.at[x_at[k], z_at[q], 1 - core], other.at[k, q], S_CORE, base + k, sibling)

    def chip_sum(k, is_far):
        places = far if is_far else near
        wait(own.at[k, places], local_sems.at[(L_OWN_FAR if is_far else L_OWN_NEAR) + k])
        wait(other.at[k, places], recv_sems.at[(R_CORE_FAR if is_far else R_CORE_NEAR) + k])
        chip[k, places] = own[k, places] + other[k, places]

    load_own(2, True)
    stats_load = pltpu.make_async_copy(stats_in, slots_in, local_sems.at[L_STATS])
    stats_load.start()
    assign_load = pltpu.make_async_copy(assign_in, assign, local_sems.at[L_ASSIGN])
    assign_load.start()
    with jax.named_scope("barrier"):
        pl.semaphore_wait(barrier, len(partners))
    in_x = (along_x(1), along_x(-1))
    in_y = (along_y(1), along_y(NY - 1))
    in_z = (along_z(1), along_z(-1))

    def tell(number, neighbours):
        for neighbour in neighbours:
            pl.semaphore_signal(in_sems.at[number], inc=1, device_id=neighbour, device_id_type=MESH)

    def hear(number):
        pl.semaphore_wait(in_sems.at[number], 2)

    tell(IN_X, in_x)
    tell(IN_Y, in_y)
    tell(IN_Z, in_z)
    for k in (2, 1, 3, 0):
        send_other(k, True)
    for k in (1, 3, 0):
        load_own(k, True)
    for k in (2, 1, 3, 0):
        load_own(k, False)
    for k in (2, 1, 3, 0):
        send_other(k, False)

    hear(IN_Y)
    tell(IN_Y + 1, in_y)
    hear(IN_Z)
    tell(IN_Z + 1, in_z)

    with jax.named_scope("chip_far"):
        chip_sum(2, True)
        hear(IN_X)
        send(chip.at[2, far, pl.ds(0, X_UNITS)], rx_far.at[0], S_X_FAR, R_X_FAR, along_x(2))
        chip_sum(1, True)
        send(chip.at[1, far, pl.ds(0, X_UNITS)], rx_far.at[1], S_X_FAR, R_X_FAR, along_x(1))
        chip_sum(3, True)
        send(chip.at[3, far, pl.ds(0, X_UNITS)], rx_far.at[2], S_X_FAR, R_X_FAR, along_x(-1))
        chip_sum(0, True)
    hear(IN_Y + 1)
    tell(IN_Y + 2, in_y)
    hear(IN_Z + 1)
    left, right = pl.ds(0, MID), pl.ds(MID, MID)
    with jax.named_scope("w_far"):
        for side, sign in enumerate((1, -1)):
            send(chip.at[:, 0, LAST, :, (left, right)[side]], rw6.at[side], S_W6, R_W6, along_z(3 * sign))
            send(chip.at[:, 1 + side, LAST], rw54.at[side, 0], S_W54, R_W54, along_z(2 * sign))
            send(chip.at[:, 3 + side, LAST], rw54.at[side, 1], S_W54, R_W54, along_z(sign))
    with jax.named_scope("chip_near"):
        chip_sum(2, False)
        chip_sum(1, False)
        chip_sum(3, False)
        chip_sum(0, False)
        for side, sign in enumerate((1, -1)):
            send(chip.at[:, 7 + side, LAST], rw_near.at[2 + side], S_W_NEAR, R_W_NEAR, along_z(2 * sign))
            send(chip.at[:, 9 + side, LAST], rw_near.at[4 + side], S_W_NEAR, R_W_NEAR, along_z(sign))
    hear(IN_Y + 2)

    my_eighth = pl.ds(pl.multiple_of(y * HALF, HALF), HALF)
    my_low = pl.ds(pl.multiple_of(MID + y * HALF, HALF), HALF)
    with jax.named_scope("slots"):
        stats_load.wait()
        slots16[...] = slots_in[...].astype(BF16)
        for d in Y_ORDER:
            top_rows = pl.ds(pl.multiple_of(y_at[d] * HALF, HALF), HALF)
            low_rows = pl.ds(pl.multiple_of(MID + y_at[d] * HALF, HALF), HALF)
            send(slots16.at[:, top_rows], slot_top.at[y], S_SLOT_TOP, R_SLOT_TOP, along_y(d))
            send(slots16.at[:, low_rows, right], slot_low.at[y], S_SLOT_LOW, R_SLOT_LOW, along_y(d))
        slot_top[y] = slots16[:, my_eighth]
        slot_low[y] = slots16[:, my_low, right]

    with jax.named_scope("x_near"):
        wait(rx_far, send_sems.at[S_X_FAR])
        for j, ref in enumerate((rx_near0, rx_near1)):
            for slot, k in enumerate((2, 1, 3)):
                send(chip.at[k, near, GROUPS[j]], ref.at[slot], S_X, R_X_NEAR + j, along_x(k if k < 3 else -1))

    rz6, rz54 = (rz6_0, rz6_1), (rz54_0, rz54_1)

    with jax.named_scope("z_far"):
        wait(rx_far, recv_sems.at[R_X_FAR])
        total = chip[0, far, pl.ds(0, X_UNITS)].astype(F32)
        for slot in range(3):
            total = total + rx_far[slot].astype(F32)
        xs[far] = total.astype(BF16)

    def send_far(j):
        units = GROUPS[j]
        for side, sign in enumerate((1, -1)):
            send(xs.at[0, units, :, (left, right)[side]], rz6[j].at[side], S_Z6 + j, R_Z6 + j, along_z(3 * sign))
            send(xs.at[1 + side, units], rz54[j].at[side, 0], S_Z54 + j, R_Z54 + j, along_z(2 * sign))
            send(xs.at[3 + side, units], rz54[j].at[side, 1], S_Z54 + j, R_Z54 + j, along_z(sign))

    send_far(0)
    with jax.named_scope("w_relay"):
        wait(rw6, recv_sems.at[R_W6])
        wait(rw54, recv_sems.at[R_W54])
        for side, sign in enumerate((1, -1)):
            total = chip[:, 5 + side, LAST].astype(F32) + rw54[side, 0].astype(F32) + rw54[side, 1].astype(F32)
            part, other_part = (left, right) if side == 0 else (right, left)
            halves = (total[:, :, :MID], total[:, :, MID:])
            tx_w[side, :, :, part] = (halves[side] + rw6[side].astype(F32)).astype(BF16)
            tx_w[side, :, :, other_part] = halves[1 - side].astype(BF16)
            send(tx_w.at[side], rw_near.at[side], S_W_NEAR, R_W_NEAR, along_z(3 * sign))

    send_far(1)

    assign_load.wait()
    owners = [assign[t] for t in range(TASKS)]
    ranks = [
        sum(((owners[s] == owners[t]).astype(jnp.int32) for s in range(t)), jnp.int32(0)) for t in range(TASKS)
    ]
    with jax.named_scope("tasks"):
        wait(slot_top.at[pl.ds(0, NY - 1)], recv_sems.at[R_SLOT_TOP])
        wait(slot_low.at[pl.ds(0, NY - 1)], recv_sems.at[R_SLOT_LOW])
        for t in range(TASKS):
            rank = jnp.minimum(ranks[t], CAP - 1)
            task_top[t, my_eighth] = slot_top[owners[t], rank]
            task_low[t, my_eighth] = slot_low[owners[t], rank]
        for d in Y_ORDER:
            send(task_top.at[:, my_eighth], task_top.at[:, my_eighth], S_TASK_TOP, R_TASK_TOP, along_y(d))
            send(task_low.at[:, my_eighth], task_low.at[:, my_eighth], S_TASK_LOW, R_TASK_LOW, along_y(d))


    rz_near = (rz_near0, rz_near1)
    rx_near = (rx_near0, rx_near1)

    def z_near(j):
        wait(rx_near[j], recv_sems.at[R_X_NEAR + j])
        total = chip[0, near, GROUPS[j]].astype(F32)
        for slot in range(3):
            total = total + rx_near[j][slot].astype(F32)
        xs[near, GROUPS[j]] = total.astype(BF16)
        xs_own[GROUPS[j]] = total[NZ - FAR - 1]

    def z_direct(j):
        for side, sign in enumerate((1, -1)):
            send(xs.at[7 + side, GROUPS[j]], rz_near[j].at[2 + side], S_Z_NEAR + j, R_Z_NEAR + j, along_z(2 * sign))
            send(xs.at[9 + side, GROUPS[j]], rz_near[j].at[4 + side], S_Z_NEAR + j, R_Z_NEAR + j, along_z(sign))

    def z_relay(j):
        units = GROUPS[j]
        for side, sign in enumerate((1, -1)):
            total = xs[5 + side, units].astype(F32)
            total = total + rz54[j][side, 0].astype(F32) + rz54[j][side, 1].astype(F32)
            part, other_part = (left, right) if side == 0 else (right, left)
            halves = (total[:, :, :MID], total[:, :, MID:])
            tx_z[side, units, :, part] = (halves[side] + rz6[j][side].astype(F32)).astype(BF16)
            tx_z[side, units, :, other_part] = halves[1 - side].astype(BF16)
            send(tx_z.at[side, units], rz_near[j].at[side], S_Z_NEAR + j, R_Z_NEAR + j, along_z(3 * sign))

    my_rows = pl.ds(pl.multiple_of(y * ROWS, ROWS), ROWS)
    my_last = pl.ds(pl.multiple_of(y * ROWS + HALF, HALF), HALF)

    def z_total(j):
        wait(rz_near[j], recv_sems.at[R_Z_NEAR + j])
        total = xs_own[GROUPS[j]]
        for n in range(6):
            total = total + rz_near[j][n].astype(F32)
        return total

    def gather(j):
        for d in Y_ORDER:
            send(grad.at[j, my_rows], grad.at[j, my_rows], S_GRAD, R_GRAD + j, along_y(d))

    with jax.named_scope("z_near0"):
        z_near(0)
    with jax.named_scope("relay0"):
        wait(rz6[0], recv_sems.at[R_Z6])
        wait(rz54[0], recv_sems.at[R_Z54])
        z_relay(0)
        z_direct(0)
    with jax.named_scope("z_near1"):
        z_near(1)
    with jax.named_scope("relay1"):
        wait(rz6[1], recv_sems.at[R_Z6 + 1])
        wait(rz54[1], recv_sems.at[R_Z54 + 1])
        z_relay(1)
        z_direct(1)
    with jax.named_scope("w_x"):
        wait(rw_near, recv_sems.at[R_W_NEAR])
        w_total = chip[:, NZ - 1, LAST].astype(F32)
        for n in range(6):
            w_total = w_total + rw_near[n].astype(F32)
        ws[...] = w_total.astype(BF16)
        for slot, k in enumerate((2, 1, 3)):
            send(ws.at[k], rw_x.at[slot], S_W_X, R_W_X, along_x(k if k < 3 else -1))
    with jax.named_scope("gather0"):
        grad[0, my_rows] = z_total(0).reshape(ROWS, BS).astype(BF16)
        gather(0)
    with jax.named_scope("gather1"):
        grad[1, pl.ds(pl.multiple_of(y * ROWS, ROWS), HALF)] = z_total(1)[0].astype(BF16)
        wait(rw_x, recv_sems.at[R_W_X])
        last = w_total[0]
        for slot in range(3):
            last = last + rw_x[slot].astype(F32)
        grad[1, my_last] = last.astype(BF16)
        gather(1)
    with jax.named_scope("task_wait"):
        wait(task_top.at[:, pl.ds(0, MID - HALF)], recv_sems.at[R_TASK_TOP])
        wait(task_low.at[:, pl.ds(0, MID - HALF)], recv_sems.at[R_TASK_LOW])
    with jax.named_scope("unfold"):
        for t in range(TASKS):
            top = DECAY_RATE * task_top[t].astype(F32)
            task_stats[t, pl.ds(0, MID)] = top
            task_stats[t, right, pl.ds(0, MID)] = top[:, MID:].T
            task_stats[t, right, right] = DECAY_RATE * task_low[t].astype(F32)

    def grams(j):
        block = grad[j]
        gram[2 * j] = dot(block, block, ((1,), (1,)))
        gram[2 * j + 1] = dot(block, block, ((0,), (0,)))

    def precondition(j):
        block = grad[j]
        left = inverse_root(task_stats[2 * j] + gram[2 * j])
        right_root = inverse_root(task_stats[2 * j + 1] + gram[2 * j + 1])
        half = dot(left, block).astype(BF16)
        pre = dot(half, right_root)
        pre_ref[...] = pre
        wide = block.astype(F32)
        scale = jnp.sqrt(jnp.sum(wide * wide) + NORM_EPSILON) / jnp.sqrt(jnp.sum(pre * pre) + NORM_EPSILON)
        upd_rows[j] = (pre_ref[my_rows] * scale).astype(BF16)

    with jax.named_scope("grad_wait0"):
        wait(grad.at[0, pl.ds(0, BS - ROWS)], recv_sems.at[R_GRAD])
    grams(0)
    precondition(0)
    with jax.named_scope("grad_wait1"):
        wait(grad.at[1, pl.ds(0, BS - ROWS)], recv_sems.at[R_GRAD + 1])
    grams(1)
    with jax.named_scope("stats_out"):
        for c in range(CAP):
            matches = [
                jnp.logical_and(owners[t] == y, ranks[t] == c).astype(jnp.int32) for t in range(TASKS)
            ]
            used = sum(matches, jnp.int32(0))
            task = sum((t * matches[t] for t in range(TASKS)), jnp.int32(0))
            fresh = DECAY_RATE * slots_in[c] + gram[jnp.minimum(task, TASKS - 1)]
            new_stats[c] = jnp.where(used > 0, fresh, jnp.zeros_like(fresh))
        stats_copy = pltpu.make_async_copy(new_stats, stats_out, local_sems.at[L_STATS_OUT])
        stats_copy.start()
    precondition(1)
    update_copy = pltpu.make_async_copy(upd_rows, update, local_sems.at[L_UPDATE])
    update_copy.start()
    with jax.named_scope("sent"):
        wait(own, send_sems.at[S_CORE])
        wait(chip.at[pl.ds(0, 3), near, pl.ds(0, X_UNITS)], send_sems.at[S_X])
        for j in range(BLOCKS):
            wait(rz6[j], send_sems.at[S_Z6 + j])
            wait(rz54[j], send_sems.at[S_Z54 + j])
        wait(rz_near0, send_sems.at[S_Z_NEAR])
        wait(rz_near1, send_sems.at[S_Z_NEAR + 1])
        wait(rw6, send_sems.at[S_W6])
        wait(rw54, send_sems.at[S_W54])
        wait(rw_near, send_sems.at[S_W_NEAR])
        wait(rw_x, send_sems.at[S_W_X])
        wait(slot_top.at[pl.ds(0, NY - 1)], send_sems.at[S_SLOT_TOP])
        wait(slot_low.at[pl.ds(0, NY - 1)], send_sems.at[S_SLOT_LOW])
        wait(task_top.at[:, pl.ds(0, MID - HALF)], send_sems.at[S_TASK_TOP])
        wait(task_low.at[:, pl.ds(0, MID - HALF)], send_sems.at[S_TASK_LOW])
        wait(grad.at[:, pl.ds(0, BS - ROWS)], send_sems.at[S_GRAD])
    with jax.named_scope("out"):
        stats_copy.wait()
        update_copy.wait()


def write_out(update_in, stats_in, update, stats_out, sems):
    copies = [
        pltpu.make_async_copy(stats_in, stats_out, sems.at[0]),
        pltpu.make_async_copy(update_in, update, sems.at[1]),
    ]
    for copy in copies:
        copy.start()
    for copy in copies:
        copy.wait()


def per_device(grad_parts, stats_in, assignment):
    parts = grad_parts.reshape(NX, NZ, NC, UNITS, HALF, BS)
    slots = stats_in[0]
    assign = assignment.reshape(TASKS)
    any_space = pl.BlockSpec(memory_space=pl.ANY)
    update, stats_out = pl.pallas_call(
        kernel,
        out_shape=(
            jax.ShapeDtypeStruct((BLOCKS, ROWS, BS), BF16),
            jax.ShapeDtypeStruct((CAP, BS, BS), F32),
        ),
        in_specs=[any_space, any_space, any_space],
        out_specs=(any_space, any_space),
        scratch_shapes=[
            pltpu.VMEM((NX, NZ, UNITS, HALF, BS), BF16),
            pltpu.VMEM((NX, NZ, UNITS, HALF, BS), BF16),
            pltpu.VMEM((NX, NZ, UNITS, HALF, BS), BF16),
            pltpu.VMEM((3, FAR, X_UNITS, HALF, BS), BF16),
            pltpu.VMEM((3, NZ - FAR, 2, HALF, BS), BF16),
            pltpu.VMEM((3, NZ - FAR, 1, HALF, BS), BF16),
            pltpu.VMEM((NZ, X_UNITS, HALF, BS), BF16),
            pltpu.VMEM((X_UNITS, HALF, BS), F32),
            pltpu.VMEM((2, 2, HALF, MID), BF16),
            pltpu.VMEM((2, 1, HALF, MID), BF16),
            pltpu.VMEM((2, 2, 2, HALF, BS), BF16),
            pltpu.VMEM((2, 2, 1, HALF, BS), BF16),
            pltpu.VMEM((2, X_UNITS, HALF, BS), BF16),
            pltpu.VMEM((6, 2, HALF, BS), BF16),
            pltpu.VMEM((6, 1, HALF, BS), BF16),
            pltpu.VMEM((2, NX, HALF, MID), BF16),
            pltpu.VMEM((2, 2, NX, HALF, BS), BF16),
            pltpu.VMEM((2, NX, HALF, BS), BF16),
            pltpu.VMEM((6, NX, HALF, BS), BF16),
            pltpu.VMEM((NX, HALF, BS), BF16),
            pltpu.VMEM((3, HALF, BS), BF16),
            pltpu.VMEM((BLOCKS, BS, BS), BF16),
            pltpu.VMEM((CAP, BS, BS), F32),
            pltpu.VMEM((CAP, BS, BS), BF16),
            pltpu.VMEM((NY, CAP, HALF, BS), BF16),
            pltpu.VMEM((NY, CAP, HALF, MID), BF16),
            pltpu.VMEM((TASKS, MID, BS), BF16),
            pltpu.VMEM((TASKS, MID, MID), BF16),
            pltpu.VMEM((TASKS, BS, BS), F32),
            pltpu.VMEM((TASKS, BS, BS), F32),
            pltpu.VMEM((CAP, BS, BS), F32),
            pltpu.VMEM((BS, BS), F32),
            pltpu.VMEM((BLOCKS, ROWS, BS), BF16),
            pltpu.SMEM((TASKS,), jnp.int32),
            pltpu.SemaphoreType.DMA((N_SEND,)),
            pltpu.SemaphoreType.DMA((N_RECV,)),
            pltpu.SemaphoreType.DMA((N_LOCAL,)),
            pltpu.SemaphoreType.REGULAR((N_IN,)),
        ],
        compiler_params=pltpu.CompilerParams(
            collective_id=0, has_side_effects=True, vmem_limit_bytes=53 * 1024 * 1024
        ),
        name="shampoo_step",
    )(parts, slots, assign)
    update, stats_out = pl.pallas_call(
        write_out,
        out_shape=(
            jax.ShapeDtypeStruct((BLOCKS, ROWS, BS), BF16),
            jax.ShapeDtypeStruct((CAP, BS, BS), F32),
        ),
        in_specs=[any_space, any_space],
        out_specs=(any_space, any_space),
        scratch_shapes=[pltpu.SemaphoreType.DMA((2,))],
        compiler_params=pltpu.CompilerParams(vmem_limit_bytes=1024 * 1024),
        name="write_out",
    )(update, stats_out)
    return update, stats_out[None]


def solution(mesh):
    in_specs = (P("dp", None, "owner", None), P("dp", "owner", None, None), P("dp", None, None))
    out_specs = (P("dp", "owner", None), P("dp", "owner", None, None))
    return jax.shard_map(
        per_device, mesh=mesh, in_specs=in_specs, out_specs=out_specs, check_vma=False
    )
```
